256 devices in a mesh: dp: 32 (over z, y), tensor: 8 (over x, core).
Axes of the slice: x: 4, y: 4, z: 8, core: 2. Of those that a mesh axis runs over, the one named last changes fastest.
Arguments:
- activations: bfloat16 [8192, 4096], P('dp'), may hold values from -6 to 6
- cotangent: bfloat16 [8192, 7168], P('dp', 'tensor'), may hold values from -0.625 to 0.625
- old_gate_up: bfloat16 [4096, 2, 28672], P('dp', None, 'tensor'), may hold values from -0.09375 to 0.09375
- kept_index: int32 [7168], replicated, may hold values from 0 to 28671, as said below
- new_slot: int32 [7168], replicated, may hold values from 0 to 7167, as said below
Outputs:
- student_gate_up: bfloat16 [4096, 2, 7168], P('dp', None, 'tensor')
- hidden: bfloat16 [8192, 7168], P('dp', 'tensor')
- weight_grad: bfloat16 [4096, 2, 7168], P('dp', None, 'tensor')
The draws below stay inside these ranges and needn't reach their ends.
Inputs may be any that keep to these rules, and one draw needn't show every extreme that they name: `kept_index`: distinct and ascending. Old owner of teacher neuron i is i // 3584. `new_slot`: A permutation; new owner of student position j is j // 896. No old owner sends more than 168 kept neurons to one new owner, and every new owner receives exactly 168 from some old owner.
All inputs are finite; a program needn't handle non-finite values.
Results may differ from the reference program's by a relative error of at most 0.024.
Values may be sent and summed in bfloat16 or wider, within the bound.
A program may use at most 128 MiB of HBM per device.

```python
import jax
import jax.numpy as jnp
from jax import lax

D = 4096
FF = 28672
KEEP = 7168
TOK_DEV = 256
TOKENS = 8192
N_DP = 32
N_TENSOR = 8


def pruning_plan(key):
    owners = N_TENSOR
    base_count = KEEP // (owners * owners)
    own_rows = FF // owners
    half_owners = owners // 2
    steps_up = base_count // 2 * (jnp.arange(half_owners, dtype=jnp.int32) + 1) // half_owners
    offsets = jnp.concatenate([steps_up, -steps_up])
    column_keys = jax.random.split(jax.random.fold_in(key, 11), owners)
    shuffles = jax.vmap(lambda one_key: jax.random.permutation(one_key, owners))(column_keys)
    pair_counts = base_count + jnp.transpose(offsets[shuffles])
    owner_counts = jnp.sum(pair_counts, axis=1)
    local_keys = jax.random.split(jax.random.fold_in(key, 12), owners)
    local_ranks = jax.vmap(lambda one_key: jax.random.permutation(one_key, own_rows))(local_keys)
    chosen = (local_ranks < owner_counts[:, None]).reshape(FF)
    kept_index = jnp.nonzero(chosen, size=KEEP)[0].astype(jnp.int32)
    old_owner = kept_index // own_rows
    first_shuffle = jax.random.permutation(jax.random.fold_in(key, 13), KEEP).astype(jnp.int32)
    first_sort = jnp.argsort(old_owner * KEEP + first_shuffle, stable=True)
    place = jnp.zeros((KEEP,), jnp.int32).at[first_sort].set(jnp.arange(KEEP, dtype=jnp.int32))
    owner_start = jnp.cumsum(owner_counts) - owner_counts
    within = place - owner_start[old_owner]
    pair_ends = jnp.cumsum(pair_counts, axis=1)
    label = jnp.sum((pair_ends[old_owner] <= within[:, None]).astype(jnp.int32), axis=1)
    second_shuffle = jax.random.permutation(jax.random.fold_in(key, 14), KEEP).astype(jnp.int32)
    second_sort = jnp.argsort(label * KEEP + second_shuffle, stable=True)
    new_slot = jnp.zeros((KEEP,), jnp.int32).at[second_sort].set(jnp.arange(KEEP, dtype=jnp.int32))
    return (kept_index, new_slot)


def draw_kept_index(key, part):
    return pruning_plan(key)[0]


def draw_new_slot(key, part):
    return pruning_plan(key)[1]


def strengthened(entries, own_key, source, target, shards_of, factor):
    def block_of(position):
        return (jnp.arange(entries.shape[position]) // (entries.shape[position] // shards_of)).reshape((-1,) + (1,) * (entries.ndim - 1 - position))

    near = jax.random.permutation(own_key, shards_of)[block_of(target)]
    other_side = (block_of(target) + shards_of // 2) % shards_of
    return jnp.where((block_of(source) == near) | (block_of(source) == other_side), factor * entries, entries)


def level_of(own_key, shape, cuts, least, largest):
    level, own = 1.0, jax.random.fold_in(own_key, 6)
    for axis_at, parts in cuts:
        draws = jnp.exp(jax.random.uniform(jax.random.fold_in(own, axis_at), (parts,), jnp.float32, least / len(cuts), largest / len(cuts)))
        level = level * jnp.repeat(draws, shape[axis_at] // parts).reshape([-1 if axis == axis_at else 1 for axis in range(len(shape))])
    return level


def normal_values(stream_key, shape, width, reach, shards=(), held_as=jnp.bfloat16):
    result = jax.random.normal(stream_key, shape, jnp.float32) * width
    if len(shards) > 0:
        result = level_of(stream_key, shape, shards, -0.22, 0.18) * result
    return jnp.clip(result, min=-reach, max=reach).astype(held_as)


def heavy_noise(stream_key, shape, deviation, bound, cuts, heavy, held_as=jnp.bfloat16):
    entries = deviation * jax.random.normal(stream_key, shape, jnp.float32)
    if cuts:
        entries = entries * level_of(stream_key, shape, cuts, -0.22, 0.18)
    return jnp.clip(strengthened(entries, jax.random.fold_in(stream_key, 3), *heavy), -bound, bound).astype(held_as)


def setup_inputs(seed: int = 0) -> dict:
    splits = jax.random.split(jax.random.key(seed), 6)
    return {
        "activations": heavy_noise(splits[0], (TOKENS, D), 1.0, 6.0, ((0, 32),), (0, 1, 32, 2.75)),
        "cotangent": normal_values(splits[1], (TOKENS, KEEP), (4.0 / TOKENS ** 0.5), 0.625, ((0, 32), (1, 8))),
        "old_gate_up": normal_values(splits[2], (D, 2, FF), D ** -0.5, 0.09375, ((0, 32), (2, 8))),
        "kept_index": draw_kept_index(jax.random.fold_in(splits[5], 71), 0),
        "new_slot": draw_new_slot(jax.random.fold_in(splits[5], 71), 0),
    }


def reference(activations, cotangent, old_gate_up, kept_index, new_slot):
    inverse_order = jnp.zeros((KEEP,), jnp.int32).at[new_slot].set(jnp.arange(KEEP, dtype=jnp.int32))
    source_neuron = kept_index[inverse_order].astype(jnp.int32)
    student_gate_up = jnp.take(old_gate_up, source_neuron, axis=2)
    gate_up = jnp.dot(activations, student_gate_up.reshape(D, 2 * KEEP), preferred_element_type=jnp.float32)
    gate_value = gate_up[:, :KEEP]
    up_value = gate_up[:, KEEP:]
    sigmoid = jax.nn.sigmoid(gate_value)
    silu_value = gate_value * sigmoid
    hidden = (silu_value * up_value).astype(jnp.bfloat16)
    incoming = cotangent.astype(jnp.float32)
    grad_gate = incoming * up_value * sigmoid * (1.0 + gate_value * (1.0 - sigmoid))
    grad_up = incoming * silu_value
    pre_grads = jnp.concatenate([grad_gate, grad_up], axis=1).astype(jnp.bfloat16)
    token_blocks = activations.reshape(N_DP, TOK_DEV, D)
    grad_blocks = pre_grads.reshape(N_DP, TOK_DEV, 2 * KEEP)

    def add_block(running, pieces):
        block_x, block_g = pieces
        partial_sum = lax.dot_general(block_x, block_g, (((0,), (0,)), ((), ())), preferred_element_type=jnp.float32)
        rounded = lax.optimization_barrier(partial_sum.astype(jnp.bfloat16))
        return running + rounded.astype(jnp.float32), None

    summed, unused = lax.scan(add_block, jnp.zeros((D, 2 * KEEP), jnp.float32), (token_blocks, grad_blocks))
    weight_grad = summed.astype(jnp.bfloat16).reshape(D, 2, KEEP)
    return student_gate_up, hidden, weight_grad
```

```python
import jax
import jax.numpy as jnp
from jax import lax
from jax.experimental import pallas as pl
from jax.experimental.pallas import tpu as pltpu
from jax.sharding import PartitionSpec as P

MESH = pl.DeviceIdType.MESH
NZ, NY, NX, NC = 8, 4, 4, 2
NT = NX * NC
D = 4096
KEEP = 7168
OWN = 896
ROWS = 3584
CAP = 176
PLACES = NT * CAP
EIGHTH = OWN // NZ
BLK = 128
TOK = NZ * BLK
CHUNK = D // NY
KB = KEEP // 128
F32 = jnp.float32
BF = jnp.bfloat16


def iota(shape, dim):
    return lax.broadcasted_iota(jnp.int32, shape, dim)


def dot(a, b):
    return lax.dot_general(a, b, (((1,), (0,)), ((), ())), preferred_element_type=F32)


def dot_nt(a, b):
    return lax.dot_general(a, b, (((1,), (1,)), ((), ())), preferred_element_type=F32)


def onehot(cond):
    return jnp.where(cond, 1.0, 0.0).astype(BF)


def interleave_matrix():
    a = iota((256, 256), 0)
    return onehot(iota((256, 256), 1) == (a & 1) * 128 + (a >> 1))


def mm(i, m=128):
    return pl.multiple_of(i, m)


class Sems:
    def __init__(self, ref):
        self.ref, self.n = ref, 0

    def take(self, count=1):
        first = self.n
        self.n += count
        return first


def kernel(act, cot, old, kept, slot, stu, hid, wg,
           a_in, c_in, o_in, krow, srow, ab, idx, ohs, inc, pb, rts, rr, stn, st2, wt, ct, cb,
           hs, hr, dg, cs, cx, pa, rb_send, rb, rc_send, rc, fg, gr,
           load_sems, send_sems, recv_sems):
    dp = lax.axis_index("dp")
    t = lax.axis_index("tensor")
    z, y = dp // NY, dp % NY
    x, c = t // NC, t % NC

    def dev(x_, c_, y_, z_):
        return (z_ * NY + y_, x_ * NC + c_)

    sib = dev(x, 1 - c, y, z)
    z_up, z_dn = dev(x, c, y, (z + 1) % NZ), dev(x, c, y, (z + NZ - 1) % NZ)
    y_up, y_dn = dev(x, c, (y + 1) % NY, z), dev(x, c, (y + NY - 1) % NY, z)

    ssem, rsem = Sems(send_sems), Sems(recv_sems)
    started = []

    def push(src, dst, recv, device):
        copy = pltpu.make_async_remote_copy(
            src_ref=src, dst_ref=dst, send_sem=send_sems.at[ssem.take()],
            recv_sem=recv_sems.at[recv], device_id=device, device_id_type=MESH)
        copy.start()
        started.append(copy)

    def arrived(dst, recv):
        pltpu.make_async_remote_copy(
            src_ref=dst, dst_ref=dst, send_sem=send_sems.at[0],
            recv_sem=recv_sems.at[recv], device_id=sib, device_id_type=MESH).wait_recv()

    loads = [
        pltpu.make_async_copy(act.at[pl.ds(mm(c * BLK), BLK), :], a_in, load_sems.at[0]),
        pltpu.make_async_copy(cot, c_in, load_sems.at[1]),
        pltpu.make_async_copy(kept, krow, load_sems.at[2]),
        pltpu.make_async_copy(slot, srow, load_sems.at[3]),
        pltpu.make_async_copy(old, o_in, load_sems.at[4]),
    ]
    for load in loads:
        load.start()

    partners = []
    for k in range(1, NT):
        tk = (t + k) % NT
        partners.append((dp, tk))
    for k in range(1, NZ):
        zk = (z + k) % NZ
        partners.append(dev(x, c, y, zk))
        partners.append(dev(x, 1 - c, y, zk))
    partners.append(y_up)
    partners.append(y_dn)
    barrier = pltpu.get_barrier_semaphore()
    for p in partners:
        pl.semaphore_signal(barrier, inc=1, device_id=p, device_id_type=MESH)

    loads[0].wait()
    for yy in range(NY):
        for zz in range(NZ):
            ab[z, :, yy * CHUNK + zz * 128:yy * CHUNK + (zz + 1) * 128] = (
                a_in[:, (zz * NY + yy) * 128:(zz * NY + yy + 1) * 128])
    pl.semaphore_wait(barrier, len(partners))

    ring_recv = [[rsem.take(), rsem.take()] for _ in range(4)]

    def ring_rows(step, way):
        if step < 4:
            return pl.ds(0, BLK)
        return pl.ds(0, BLK // 2) if way == 0 else pl.ds(BLK // 2, BLK // 2)

    def ring_send(step):
        for way in range(2):
            block = (z + NZ - (step - 1)) % NZ if way == 0 else (z + step - 1) % NZ
            rows = ring_rows(step, way)
            push(ab.at[block, rows, :], ab.at[block, rows, :], ring_recv[step - 1][way],
                 z_up if way == 0 else z_dn)

    def ring_wait(step):
        for way in range(2):
            block = (z + NZ - step) % NZ if way == 0 else (z + step) % NZ
            arrived(ab.at[block, ring_rows(step, way), :], ring_recv[step - 1][way])

    ring_send(1)

    loads[1].wait()
    ct[...] = c_in[...].astype(F32).T.astype(BF)
    cot_recv = rsem.take(NZ * NC)
    cot_slot = cot_recv + z * NC + c
    for k in range(NZ):
        zk = (z + k) % NZ
        for e in range(NC):
            ck = (c + e) % NC
            src = ct.at[pl.ds(mm(zk * EIGHTH, 16), EIGHTH), pl.ds(mm(ck * BLK), BLK)]
            dst = cb.at[c, :, pl.ds(mm(z * BLK), BLK)]
            if k == 0 and e == 0:
                own = pltpu.make_async_copy(src, dst, load_sems.at[5])
                own.start()
                own.wait()
            else:
                push(src, dst, cot_slot, dev(x, ck, y, zk))

    loads[2].wait()
    loads[3].wait()
    kv, sv = krow[...], srow[...]
    o, j = jnp.zeros_like(kv), jnp.zeros_like(sv)
    for i in range(1, NT):
        o = o + jnp.where(kv >= ROWS * i, 1, 0)
        j = j + jnp.where(sv >= OWN * i, 1, 0)
    idx[0:1, :] = jnp.where(o == t, j, 99)
    idx[1:2, :] = jnp.where(j == t, o + 8, 99)
    row16 = iota((16, 128), 0)
    for b in range(KB):
        lanes = slice(b * 128, (b + 1) * 128)
        key = jnp.where(row16 < 8, jnp.broadcast_to(idx[0:1, lanes], (16, 128)),
                        jnp.broadcast_to(idx[1:2, lanes], (16, 128)))
        ohs[b * 16:(b + 1) * 16, :] = onehot(key == row16)
    upto = onehot(iota((128, 128), 0) <= iota((128, 128), 1))
    inc[...] = dot(ohs[...], upto)
    run = jnp.zeros((16, 1), F32)
    for b in range(KB):
        lanes = slice(b * 128, (b + 1) * 128)
        here = inc[b * 16:(b + 1) * 16, :]
        rank = ohs[b * 16:(b + 1) * 16, :].astype(F32) * (here + run)
        rank_s = jnp.sum(rank[0:8], axis=0, keepdims=True).astype(jnp.int32)
        rank_r = jnp.sum(rank[8:16], axis=0, keepdims=True).astype(jnp.int32)
        dest, source = idx[0:1, lanes], idx[1:2, lanes]
        idx[2:3, lanes] = jnp.where(dest < 99, dest * CAP + rank_s, 0)
        idx[3:4, lanes] = jnp.where(source < 99, (source - 8) * CAP + rank_r, 0)
        run = run + here[:, 127:128]
    idx[4:5, :] = kv - t * ROWS
    idx[5:6, :] = sv - t * OWN

    def scatter(step, carry):
        by_neuron, by_slot = carry
        lanes = pl.ds(mm(step * OWN), OWN)
        vs, vr, ln, ls = (idx[i:i + 1, lanes] for i in (2, 3, 4, 5))
        high = iota((32, OWN), 0) == (ln >> 7)
        values = jnp.concatenate([
            jnp.where(high, vs >> 7, 0), jnp.where(high, vs & 127, 0)], axis=0)
        low = onehot(iota((128, OWN), 0) == (ln & 127))
        by_neuron = by_neuron + dot_nt(values.astype(F32).astype(BF), low)
        high = iota((8, OWN), 0) == (ls >> 7)
        values = jnp.concatenate([
            jnp.where(high, vr >> 7, 0), jnp.where(high, vr & 127, 0)], axis=0)
        low = onehot(iota((128, OWN), 0) == (ls & 127))
        by_slot = by_slot + dot_nt(low, values.astype(F32).astype(BF))
        return by_neuron, by_slot

    by_neuron, by_slot = lax.fori_loop(
        0, KEEP // OWN, scatter, (jnp.zeros((64, 128), F32), jnp.zeros((128, 16), F32)))
    place_s = (by_neuron[0:32] * 128.0 + by_neuron[32:64]).astype(jnp.int32)
    place_r = (by_slot[:, 0:8] * 128.0 + by_slot[:, 8:16]).astype(jnp.int32)

    loads[4].wait()
    own_recv = rsem.take(NT)
    own_send = ssem.take(NT)

    def own_copy(to):
        return pltpu.make_async_remote_copy(
            src_ref=rts.at[to], dst_ref=rr.at[pl.ds(mm(t * CAP, 16), CAP), :],
            send_sem=send_sems.at[own_send + to], recv_sem=recv_sems.at[own_recv + t],
            device_id=(dp, to), device_id_type=MESH)

    def select(k, _):
        to = (t + k) % NT
        row = iota((CAP, 128), 0) + (to * CAP + 1)
        for h in range(ROWS // 128):
            pb[:, h * 128:(h + 1) * 128] = onehot(place_s[h:h + 1, :] == row)
        rts[to] = dot_nt(pb[...], o_in[...]).astype(BF)

        @pl.when(k < NT)
        def _():
            own_copy(to).start()
        return 0

    lax.fori_loop(1, NT + 1, select, 0)
    rr[pl.ds(mm(t * CAP, 16), CAP), :] = rts[t]

    ring_wait(1)
    ring_send(2)

    for k in range(1, NT):
        frm = (t + k) % NT
        arrived(rr.at[pl.ds(mm(frm * CAP, 16), CAP), :], own_recv + frm)
    pi = interleave_matrix()
    got = rr[...]
    for h in range(OWN // 128):
        q = onehot(iota((128, PLACES), 1) + 1 == place_r[:, h:h + 1])
        mine = dot(q, got).astype(BF)
        stn[h * 128:(h + 1) * 128, :] = mine
        split = dot(mine, pi).astype(BF)
        st2[0, h * 128:(h + 1) * 128, :] = split[:, 0:128]
        st2[1, h * 128:(h + 1) * 128, :] = split[:, 128:256]

    w_recv = rsem.take(NZ)
    for k in range(NZ):
        zk = (z + k) % NZ
        src = st2.at[:, pl.ds(mm(zk * EIGHTH, 16), EIGHTH), :]
        dst = wt.at[c, y, :, :, pl.ds(mm(z * 128), 128)]
        if k == 0:
            own = pltpu.make_async_copy(src, dst, load_sems.at[5])
            own.start()
            own.wait()
        else:
            push(src, dst, w_recv + z, dev(x, c, y, zk))

    stu[...] = stn[...].astype(F32).T.astype(BF)

    ring_wait(2)
    ring_send(3)

    for k in range(1, NZ):
        zk = (z + k) % NZ
        arrived(wt.at[c, y, :, :, pl.ds(mm(zk * 128), 128)], w_recv + zk)

    y1, y3, y2 = (y + 1) % NY, (y + 3) % NY, (y + 2) % NY
    wy = [rsem.take() for _ in range(4)]
    core_recv = rsem.take(NY)

    def to_core(yy):
        push(wt.at[c, yy], wt.at[c, yy], core_recv + yy, sib)

    push(wt.at[c, y], wt.at[c, y], wy[0], y_up)
    push(wt.at[c, y], wt.at[c, y], wy[1], y_dn)
    to_core(y)
    ring_wait(3)
    ring_send(4)
    arrived(wt.at[c, y3], wy[0])
    push(wt.at[c, y3, 0], wt.at[c, y3, 0], wy[2], y_up)
    arrived(wt.at[c, y1], wy[1])
    push(wt.at[c, y1, 1], wt.at[c, y1, 1], wy[3], y_dn)
    to_core(y3)
    to_core(y1)
    arrived(wt.at[c, y2, 0], wy[2])
    arrived(wt.at[c, y2, 1], wy[3])
    to_core(y2)

    for k in range(NZ):
        zk = (z + k) % NZ
        for e in range(NC):
            if k == 0 and e == 0:
                continue
            ck = (c + e) % NC
            arrived(cb.at[ck, :, pl.ds(mm(zk * BLK), BLK)], cot_recv + zk * NC + ck)
    for k in range(NY):
        yy = (y + k) % NY
        arrived(wt.at[1 - c, yy], core_recv + yy)
    ring_wait(4)

    def forward(pair, _):
        lanes = pl.ds(mm(pair * 256), 256)
        tokens = ab[pl.ds(pair * 2, 2)].reshape(256, D)
        total = jnp.zeros((448, 256), F32)
        for yy in range(NY):
            total = total + dot_nt(wt[:, yy].reshape(448, CHUNK),
                                   tokens[:, yy * CHUNK:(yy + 1) * CHUNK])
        for cc in range(NC):
            gate = total[cc * 224:cc * 224 + 112]
            up = total[cc * 224 + 112:cc * 224 + 224]
            sig = jax.nn.sigmoid(gate)
            silu = gate * sig
            hs[cc, :, lanes] = (silu * up).astype(BF)
            incoming = cb[cc, :, lanes].astype(F32)
            dg[cc, 0:112, lanes] = (incoming * up * sig * (1.0 + gate * (1.0 - sig))).astype(BF)
            dg[cc, 112:224, lanes] = (incoming * silu).astype(BF)
        return 0

    lax.fori_loop(0, NZ // 2, forward, 0)

    hid_recv = rsem.take(NZ * NC)
    for k in range(NZ):
        zk = (z + k) % NZ
        for e in range(NC):
            ck = (c + e) % NC
            src = hs.at[ck, :, pl.ds(mm(zk * BLK), BLK)]
            dst = hr.at[pl.ds(mm(z * EIGHTH, 16), EIGHTH), pl.ds(mm(c * BLK), BLK)]
            if k == 0 and e == 0:
                own = pltpu.make_async_copy(src, dst, load_sems.at[5])
                own.start()
                own.wait()
            else:
                push(src, dst, hid_recv + z * NC + c, dev(x, ck, y, zk))

    order = [y2, y1, y3, y]
    core_sum = [rsem.take() for _ in range(4)]
    for n, yy in enumerate(order):
        def part(s, _, n=n, yy=yy):
            lanes = pl.ds(mm(s * 256), 256)
            width = ab[:, :, pl.ds(mm(yy * CHUNK + s * 256), 256)].reshape(TOK, 256)
            cs[n, :, :, lanes] = dot(dg[1 - c], width).astype(BF).reshape(2, EIGHTH, 256)
            pa[n, :, :, lanes] = dot(dg[c], width).reshape(2, EIGHTH, 256)
            return 0
        lax.fori_loop(0, CHUNK // 256, part, 0)
        push(cs.at[n], cx.at[n], core_sum[n], sib)

    sem_b = [rsem.take(), rsem.take()]
    sem_c = [rsem.take(), rsem.take()]
    arrived(cx.at[0], core_sum[0])
    rb_send[...] = (pa[0] + cx[0].astype(F32)).astype(BF)
    push(rb_send.at[0], rb.at[0], sem_b[0], y_up)
    push(rb_send.at[1], rb.at[1], sem_b[1], y_dn)
    for way in range(2):
        n = 1 + way
        arrived(cx.at[n], core_sum[n])
        arrived(rb.at[way], sem_b[way])
        rc_send[way, way] = (pa[n, way] + cx[n, way].astype(F32) + rb[way].astype(F32)).astype(BF)
        rc_send[way, 1 - way] = (pa[n, 1 - way] + cx[n, 1 - way].astype(F32)).astype(BF)
        push(rc_send.at[way], rc.at[way], sem_c[way], y_up if way == 0 else y_dn)
    arrived(cx.at[3], core_sum[3])

    for k in range(NZ):
        zk = (z + k) % NZ
        for e in range(NC):
            if k == 0 and e == 0:
                continue
            ck = (c + e) % NC
            arrived(hr.at[pl.ds(mm(zk * EIGHTH, 16), EIGHTH), pl.ds(mm(ck * BLK), BLK)],
                    hid_recv + zk * NC + ck)
    hid[...] = hr[...].astype(F32).T.astype(BF)

    arrived(rc.at[0], sem_c[0])
    arrived(rc.at[1], sem_c[1])
    fg[...] = (pa[3] + cx[3].astype(F32) + rc[0].astype(F32) + rc[1].astype(F32)).astype(BF)

    g_recv = rsem.take(NZ)
    for k in range(NZ):
        zk = (z + k) % NZ
        src = fg.at[:, :, pl.ds(mm(zk * 128), 128)]
        dst = gr.at[:, pl.ds(mm(z * EIGHTH, 16), EIGHTH), :]
        if k == 0:
            own = pltpu.make_async_copy(src, dst, load_sems.at[5])
            own.start()
            own.wait()
        else:
            push(src, dst, g_recv + z, dev(x, c, y, zk))
    for k in range(1, NZ):
        zk = (z + k) % NZ
        arrived(gr.at[:, pl.ds(mm(zk * EIGHTH, 16), EIGHTH), :], g_recv + zk)
    both = jnp.concatenate([gr[0], gr[1]], axis=1)
    wg[...] = dot_nt(interleave_matrix(), both).astype(BF)

    def drain(k, _):
        own_copy((t + k) % NT).wait_send()
        return 0

    lax.fori_loop(1, NT, drain, 0)
    for copy in started:
        copy.wait_send()
    assert ssem.n <= send_sems.shape[0] and rsem.n <= recv_sems.shape[0], (ssem.n, rsem.n)


def per_device(activations, cotangent, old_gate_up, kept_index, new_slot):
    any_ = pl.BlockSpec(memory_space=pl.ANY)
    vmem = pl.BlockSpec(memory_space=pltpu.VMEM)
    V = pltpu.VMEM
    student, hidden, grad = pl.pallas_call(
        kernel,
        out_shape=(
            jax.ShapeDtypeStruct((256, OWN), BF),
            jax.ShapeDtypeStruct((256, OWN), BF),
            jax.ShapeDtypeStruct((256, OWN), BF),
        ),
        in_specs=[any_] * 5,
        out_specs=(vmem, vmem, vmem),
        scratch_shapes=[
            V((BLK, D), BF),
            V((256, OWN), BF),
            V((256, ROWS), BF),
            V((1, KEEP), jnp.int32),
            V((1, KEEP), jnp.int32),
            V((NZ, BLK, D), BF),
            V((8, KEEP), jnp.int32),
            V((KB * 16, 128), BF),
            V((KB * 16, 128), F32),
            V((CAP, ROWS), BF),
            V((NT, CAP, 256), BF),
            V((PLACES, 256), BF),
            V((OWN, 256), BF),
            V((2, OWN, 128), BF),
            V((NC, NY, 2, EIGHTH, CHUNK), BF),
            V((OWN, 256), BF),
            V((NC, EIGHTH, TOK), BF),
            V((NC, EIGHTH, TOK), BF),
            V((OWN, 256), BF),
            V((NC, 2 * EIGHTH, TOK), BF),
            V((NY, 2, EIGHTH, CHUNK), BF),
            V((NY, 2, EIGHTH, CHUNK), BF),
            V((NY, 2, EIGHTH, CHUNK), F32),
            V((2, EIGHTH, CHUNK), BF),
            V((2, EIGHTH, CHUNK), BF),
            V((2, 2, EIGHTH, CHUNK), BF),
            V((2, 2, EIGHTH, CHUNK), BF),
            V((2, EIGHTH, CHUNK), BF),
            V((2, OWN, 128), BF),
            pltpu.SemaphoreType.DMA((6,)),
            pltpu.SemaphoreType.DMA((96,)),
            pltpu.SemaphoreType.DMA((96,)),
        ],
        compiler_params=pltpu.CompilerParams(
            collective_id=0, has_side_effects=True, vmem_limit_bytes=60 * 1024 * 1024),
        cost_estimate=pl.CostEstimate(flops=12_000_000_000, bytes_accessed=8_000_000, transcendentals=1_000_000),
        name="student_projection",
    )(activations, cotangent, old_gate_up.reshape(256, ROWS),
      kept_index.reshape(1, KEEP), new_slot.reshape(1, KEEP))
    return student.reshape(128, 2, OWN), hidden, grad.reshape(128, 2, OWN)


def solution(mesh):
    placed = (P("dp", None), P("dp", "tensor"), P("dp", None, "tensor"), P(), P())
    return jax.shard_map(
        per_device,
        mesh=mesh,
        in_specs=placed,
        out_specs=(P("dp", None, "tensor"), P("dp", "tensor"), P("dp", None, "tensor")),
        check_vma=False,
    )
```

```python
import jax
import jax.numpy as jnp
from jax import lax
from jax.experimental import pallas as pl
from jax.experimental.pallas import tpu as pltpu
from jax.sharding import PartitionSpec as P

MESH = pl.DeviceIdType.MESH
NZ, NY, NX, NC = 8, 4, 4, 2
NT = NX * NC
D = 4096
KEEP = 7168
OWN = 896
ROWS = 3584
CAP = 176
PLACES = NT * CAP
EIGHTH = OWN // NZ
BLK = 128
TOK = NZ * BLK
CHUNK = D // NY
DIRECT = 1024
SHARE = (D - DIRECT) // NX
HALF = BLK // 2
KB = KEEP // 128
F32 = jnp.float32
BF = jnp.bfloat16


def iota(shape, dim):
    return lax.broadcasted_iota(jnp.int32, shape, dim)


def dot(a, b):
    return lax.dot_general(a, b, (((1,), (0,)), ((), ())), preferred_element_type=F32)


def dot_nt(a, b):
    return lax.dot_general(a, b, (((1,), (1,)), ((), ())), preferred_element_type=F32)


def onehot(cond):
    return jnp.where(cond, 1.0, 0.0).astype(BF)


def interleave_matrix():
    a = iota((256, 256), 0)
    return onehot(iota((256, 256), 1) == (a & 1) * 128 + (a >> 1))


def mm(i, m=128):
    return pl.multiple_of(i, m)


class Sems:
    def __init__(self, ref):
        self.ref, self.n = ref, 0

    def take(self, count=1):
        first = self.n
        self.n += count
        return first


def kernel(act, cot, old, kept, slot, stu, hid, wg,
           a_in, c_in, o_in, krow, srow, ab, idx, ohs, inc, pb, rts, rr, stn, st2, wt, ct, cb,
           hs, hr, dg, cs, cx, pa, rb_send, rb, rc_send, rc, fg, gr,
           load_sems, send_sems, recv_sems):
    dp = lax.axis_index("dp")
    t = lax.axis_index("tensor")
    z, y = dp // NY, dp % NY
    x, c = t // NC, t % NC

    def dev(x_, c_, y_, z_):
        return (z_ * NY + y_, x_ * NC + c_)

    sib = dev(x, 1 - c, y, z)
    z_up, z_dn = dev(x, c, y, (z + 1) % NZ), dev(x, c, y, (z + NZ - 1) % NZ)
    y_up, y_dn = dev(x, c, (y + 1) % NY, z), dev(x, c, (y + NY - 1) % NY, z)
    x_up, x_dn = dev((x + 1) % NX, c, y, z), dev((x + NX - 1) % NX, c, y, z)

    ssem, rsem = Sems(send_sems), Sems(recv_sems)
    started = []

    def push(src, dst, recv, device):
        copy = pltpu.make_async_remote_copy(
            src_ref=src, dst_ref=dst, send_sem=send_sems.at[ssem.take()],
            recv_sem=recv_sems.at[recv], device_id=device, device_id_type=MESH)
        copy.start()
        started.append(copy)

    def arrived(dst, recv):
        pltpu.make_async_remote_copy(
            src_ref=dst, dst_ref=dst, send_sem=send_sems.at[0],
            recv_sem=recv_sems.at[recv], device_id=sib, device_id_type=MESH).wait_recv()

    loads = [
        pltpu.make_async_copy(act.at[pl.ds(mm(c * BLK), BLK), :], a_in, load_sems.at[0]),
        pltpu.make_async_copy(cot, c_in, load_sems.at[1]),
        pltpu.make_async_copy(kept, krow, load_sems.at[2]),
        pltpu.make_async_copy(slot, srow, load_sems.at[3]),
        pltpu.make_async_copy(old, o_in, load_sems.at[4]),
    ]
    for load in loads:
        load.start()

    partners = []
    for k in range(1, NT):
        tk = (t + k) % NT
        partners.append((dp, tk))
    for k in range(1, NZ):
        zk = (z + k) % NZ
        partners.append(dev(x, c, y, zk))
        partners.append(dev(x, 1 - c, y, zk))
    partners.append(y_up)
    partners.append(y_dn)
    barrier = pltpu.get_barrier_semaphore()
    for p in partners:
        pl.semaphore_signal(barrier, inc=1, device_id=p, device_id_type=MESH)

    loads[0].wait()
    for yy in range(NY):
        for zz in range(NZ):
            ab[z, :, yy * CHUNK + zz * 128:yy * CHUNK + (zz + 1) * 128] = (
                a_in[:, (zz * NY + yy) * 128:(zz * NY + yy + 1) * 128])
    pl.semaphore_wait(barrier, len(partners))

    def share(xx):
        return pl.ds(mm(DIRECT + xx % NX * SHARE), SHARE)

    regions = [share(x), pl.ds(0, DIRECT)]
    ring_recv = [[[rsem.take(), rsem.take()] for _ in range(2)] for _ in range(4)]
    hand_recv = [[rsem.take(4), rsem.take(4)] for _ in range(4)]

    def ring_block(step, way):
        return (z + NZ - step) % NZ if way == 0 else (z + step) % NZ

    def ring_rows(step, way):
        if step < 4:
            return pl.ds(0, BLK)
        return pl.ds(0, HALF) if way == 0 else pl.ds(HALF, HALF)

    def ring_send(step, r):
        for way in range(2):
            piece = ab.at[ring_block(step - 1, way), ring_rows(step, way), regions[r]]
            push(piece, piece, ring_recv[step - 1][way][r], z_up if way == 0 else z_dn)

    def ring_wait(step, r):
        for way in range(2):
            arrived(ab.at[ring_block(step, way), ring_rows(step, way), regions[r]],
                    ring_recv[step - 1][way][r])

    def hand_blocks(step):
        return [(ring_block(step, way), hand_recv[step - 1][way]) for way in range(2 if step < 4 else 1)]

    def hand_on(step):
        for block, sem in hand_blocks(step):
            piece = ab.at[block, :, share(x)]
            push(piece, piece, sem, x_up)
            push(piece, piece, sem + 1, x_dn)

    def relay(step):
        for block, sem in hand_blocks(step):
            arrived(ab.at[block, :, share(x + 3)], sem)
            piece = ab.at[block, pl.ds(0, HALF), share(x + 3)]
            push(piece, piece, sem + 2, x_up)
            arrived(ab.at[block, :, share(x + 1)], sem + 1)
            piece = ab.at[block, pl.ds(HALF, HALF), share(x + 1)]
            push(piece, piece, sem + 3, x_dn)

    def handed(step):
        for block, sem in hand_blocks(step):
            arrived(ab.at[block, pl.ds(0, HALF), share(x + 2)], sem + 2)
            arrived(ab.at[block, pl.ds(HALF, HALF), share(x + 2)], sem + 3)

    def ring(step):
        for r in range(2):
            ring_wait(step, r)
            if step < 4:
                ring_send(step + 1, r)
            if r == 0:
                hand_on(step)

    ring_send(1, 0)
    ring_send(1, 1)

    loads[1].wait()
    ct[...] = c_in[...].astype(F32).T.astype(BF)
    cot_recv = rsem.take(NZ * NC)
    cot_slot = cot_recv + z * NC + c
    for k in range(NZ):
        zk = (z + k) % NZ
        for e in range(NC):
            ck = (c + e) % NC
            src = ct.at[pl.ds(mm(zk * EIGHTH, 16), EIGHTH), pl.ds(mm(ck * BLK), BLK)]
            dst = cb.at[c, :, pl.ds(mm(z * BLK), BLK)]
            if k == 0 and e == 0:
                own = pltpu.make_async_copy(src, dst, load_sems.at[5])
                own.start()
                own.wait()
            else:
                push(src, dst, cot_slot, dev(x, ck, y, zk))

    loads[2].wait()
    loads[3].wait()
    kv, sv = krow[...], srow[...]
    o, j = jnp.zeros_like(kv), jnp.zeros_like(sv)
    for i in range(1, NT):
        o = o + jnp.where(kv >= ROWS * i, 1, 0)
        j = j + jnp.where(sv >= OWN * i, 1, 0)
    idx[0:1, :] = jnp.where(o == t, j, 99)
    idx[1:2, :] = jnp.where(j == t, o + 8, 99)
    row16 = iota((16, 128), 0)
    for b in range(KB):
        lanes = slice(b * 128, (b + 1) * 128)
        key = jnp.where(row16 < 8, jnp.broadcast_to(idx[0:1, lanes], (16, 128)),
                        jnp.broadcast_to(idx[1:2, lanes], (16, 128)))
        ohs[b * 16:(b + 1) * 16, :] = onehot(key == row16)
    upto = onehot(iota((128, 128), 0) <= iota((128, 128), 1))
    inc[...] = dot(ohs[...], upto)
    run = jnp.zeros((16, 1), F32)
    for b in range(KB):
        lanes = slice(b * 128, (b + 1) * 128)
        here = inc[b * 16:(b + 1) * 16, :]
        rank = ohs[b * 16:(b + 1) * 16, :].astype(F32) * (here + run)
        rank_s = jnp.sum(rank[0:8], axis=0, keepdims=True).astype(jnp.int32)
        rank_r = jnp.sum(rank[8:16], axis=0, keepdims=True).astype(jnp.int32)
        dest, source = idx[0:1, lanes], idx[1:2, lanes]
        idx[2:3, lanes] = jnp.where(dest < 99, dest * CAP + rank_s, 0)
        idx[3:4, lanes] = jnp.where(source < 99, (source - 8) * CAP + rank_r, 0)
        run = run + here[:, 127:128]
    idx[4:5, :] = kv - t * ROWS
    idx[5:6, :] = sv - t * OWN

    def scatter(step, carry):
        by_neuron, by_slot = carry
        lanes = pl.ds(mm(step * OWN), OWN)
        vs, vr, ln, ls = (idx[i:i + 1, lanes] for i in (2, 3, 4, 5))
        high = iota((32, OWN), 0) == (ln >> 7)
        values = jnp.concatenate([
            jnp.where(high, vs >> 7, 0), jnp.where(high, vs & 127, 0)], axis=0)
        low = onehot(iota((128, OWN), 0) == (ln & 127))
        by_neuron = by_neuron + dot_nt(values.astype(F32).astype(BF), low)
        high = iota((8, OWN), 0) == (ls >> 7)
        values = jnp.concatenate([
            jnp.where(high, vr >> 7, 0), jnp.where(high, vr & 127, 0)], axis=0)
        low = onehot(iota((128, OWN), 0) == (ls & 127))
        by_slot = by_slot + dot_nt(low, values.astype(F32).astype(BF))
        return by_neuron, by_slot

    by_neuron, by_slot = lax.fori_loop(
        0, KEEP // OWN, scatter, (jnp.zeros((64, 128), F32), jnp.zeros((128, 16), F32)))
    place_s = (by_neuron[0:32] * 128.0 + by_neuron[32:64]).astype(jnp.int32)
    place_r = (by_slot[:, 0:8] * 128.0 + by_slot[:, 8:16]).astype(jnp.int32)

    loads[4].wait()
    own_recv = rsem.take(NT)
    own_send = ssem.take(NT)

    def own_copy(to):
        return pltpu.make_async_remote_copy(
            src_ref=rts.at[to], dst_ref=rr.at[pl.ds(mm(t * CAP, 16), CAP), :],
            send_sem=send_sems.at[own_send + to], recv_sem=recv_sems.at[own_recv + t],
            device_id=(dp, to), device_id_type=MESH)

    def select(k, _):
        to = (t + k) % NT
        row = iota((CAP, 128), 0) + (to * CAP + 1)
        for h in range(ROWS // 128):
            pb[:, h * 128:(h + 1) * 128] = onehot(place_s[h:h + 1, :] == row)
        rts[to] = dot_nt(pb[...], o_in[...]).astype(BF)

        @pl.when(k < NT)
        def _():
            own_copy(to).start()
        return 0

    lax.fori_loop(1, NT + 1, select, 0)
    rr[pl.ds(mm(t * CAP, 16), CAP), :] = rts[t]

    ring(1)

    for k in range(1, NT):
        frm = (t + k) % NT
        arrived(rr.at[pl.ds(mm(frm * CAP, 16), CAP), :], own_recv + frm)
    pi = interleave_matrix()
    got = rr[...]
    for h in range(OWN // 128):
        q = onehot(iota((128, PLACES), 1) + 1 == place_r[:, h:h + 1])
        mine = dot(q, got).astype(BF)
        stn[h * 128:(h + 1) * 128, :] = mine
        split = dot(mine, pi).astype(BF)
        st2[0, h * 128:(h + 1) * 128, :] = split[:, 0:128]
        st2[1, h * 128:(h + 1) * 128, :] = split[:, 128:256]

    w_recv = rsem.take(NZ)

    def eighth(k):
        zk = (z + k) % NZ
        return (st2.at[:, pl.ds(mm(zk * EIGHTH, 16), EIGHTH), :],
                wt.at[c, y, :, :, pl.ds(mm(z * 128), 128)], dev(x, c, y, zk))

    own = pltpu.make_async_copy(*eighth(0)[:2], load_sems.at[5])
    own.start()
    for k in (1, 7, 2, 6, 3, 5, 4):
        src, dst, to = eighth(k)
        push(src, dst, w_recv + z, to)
    own.wait()

    stu[...] = stn[...].astype(F32).T.astype(BF)

    relay(1)
    ring(2)

    y1, y3, y2 = (y + 1) % NY, (y + 3) % NY, (y + 2) % NY
    pairs = [(z // 2 + k) % (NZ // 2) for k in (0, 1, 3, 2)]
    wy = [rsem.take(4) for _ in pairs]
    core_recv = rsem.take(NY * len(pairs))

    def w_part(cc, yy, pair):
        return wt.at[cc, yy, :, :, pl.ds(mm(pair * 256, 256), 256)]

    def w_half(yy, g, pair):
        return wt.at[c, yy, g, :, pl.ds(mm(pair * 256, 256), 256)]

    def to_core(yy, pair):
        push(w_part(c, yy, pair), w_part(c, yy, pair), core_recv + pair * NY + yy, sib)

    for n, pair in enumerate(pairs):
        for zk in ([z + 1 - 2 * (z % 2)] if n == 0 else [pair * 2, pair * 2 + 1]):
            arrived(wt.at[c, y, :, :, pl.ds(mm(zk * 128), 128)], w_recv + zk)
        push(w_part(c, y, pair), w_part(c, y, pair), wy[n], y_up)
        push(w_part(c, y, pair), w_part(c, y, pair), wy[n] + 1, y_dn)
        to_core(y, pair)
    relay(2)
    ring(3)
    for n, pair in enumerate(pairs):
        arrived(w_part(c, y3, pair), wy[n])
        push(w_half(y3, 0, pair), w_half(y3, 0, pair), wy[n] + 2, y_up)
        arrived(w_part(c, y1, pair), wy[n] + 1)
        push(w_half(y1, 1, pair), w_half(y1, 1, pair), wy[n] + 3, y_dn)
        to_core(y3, pair)
        to_core(y1, pair)
    relay(3)
    for n, pair in enumerate(pairs):
        arrived(w_half(y2, 0, pair), wy[n] + 2)
        arrived(w_half(y2, 1, pair), wy[n] + 3)
        to_core(y2, pair)
    ring(4)

    for k in range(NZ):
        zk = (z + k) % NZ
        for e in range(NC):
            if k == 0 and e == 0:
                continue
            ck = (c + e) % NC
            arrived(cb.at[ck, :, pl.ds(mm(zk * BLK), BLK)], cot_recv + zk * NC + ck)
    for pair in pairs:
        for yy in (y, y3, y1, y2):
            arrived(w_part(1 - c, yy, pair), core_recv + pair * NY + yy)

    hid_recv = rsem.take(NZ * NC)

    def forward(blocks):
        tokens = jnp.concatenate([ab[b] for b in blocks], axis=0)
        total = jnp.zeros((448, 256), F32)
        for yy in range(NY):
            total = total + dot_nt(wt[:, yy].reshape(448, CHUNK),
                                   tokens[:, yy * CHUNK:(yy + 1) * CHUNK])
        for cc in range(NC):
            for i, b in enumerate(blocks):
                lanes = pl.ds(mm(b * BLK), BLK)
                gate = total[cc * 224:cc * 224 + 112, i * BLK:(i + 1) * BLK]
                up = total[cc * 224 + 112:cc * 224 + 224, i * BLK:(i + 1) * BLK]
                sig = jax.nn.sigmoid(gate)
                silu = gate * sig
                hs[cc, :, lanes] = (silu * up).astype(BF)
                incoming = cb[cc, :, lanes].astype(F32)
                dg[cc, 0:112, lanes] = (incoming * up * sig * (1.0 + gate * (1.0 - sig))).astype(BF)
                dg[cc, 112:224, lanes] = (incoming * silu).astype(BF)

    def hidden_out(k):
        zk = (z + k) % NZ
        for e in range(NC):
            ck = (c + e) % NC
            src = hs.at[ck, :, pl.ds(mm(zk * BLK), BLK)]
            dst = hr.at[pl.ds(mm(z * EIGHTH, 16), EIGHTH), pl.ds(mm(c * BLK), BLK)]
            if k == 0 and e == 0:
                own = pltpu.make_async_copy(src, dst, load_sems.at[5])
                own.start()
                own.wait()
            else:
                push(src, dst, hid_recv + z * NC + c, dev(x, ck, y, zk))

    for step in (1, 2, 3):
        handed(step)
        forward([ring_block(step, 0), ring_block(step, 1)])
        hidden_out(NZ - step)
        hidden_out(step)
        if step == 2:
            relay(4)
    handed(4)
    forward([z, ring_block(4, 0)])
    hidden_out(4)
    hidden_out(0)

    order = [y2, y1, y3, y]
    parts = [(z // 2 + k) % (NZ // 2) for k in (2, 1, 3, 0)]
    core_sum = [[rsem.take() for _ in order] for _ in parts]
    sem_b = [[rsem.take(), rsem.take()] for _ in parts]
    sem_c = [[rsem.take(), rsem.take()] for _ in parts]
    g_recv = rsem.take(NZ)

    def lanes_of(pair):
        return pl.ds(mm(pair * 256, 256), 256)

    def gradient(p):
        for n, yy in enumerate(order):
            width = ab[:, :, pl.ds(mm(yy * CHUNK + parts[p] * 256, 256), 256)].reshape(TOK, 256)
            cs[p, n] = dot(dg[1 - c], width).astype(BF).reshape(2, EIGHTH, 256)
            push(cs.at[p, n], cx.at[p, n], core_sum[p][n], sib)
            pa[p, n] = dot(dg[c], width).reshape(2, EIGHTH, 256)

    def send_b(p):
        arrived(cx.at[p, 0], core_sum[p][0])
        rb_send[p] = (pa[p, 0] + cx[p, 0].astype(F32)).astype(BF)
        push(rb_send.at[p, 0], rb.at[p, 0], sem_b[p][0], y_up)
        push(rb_send.at[p, 1], rb.at[p, 1], sem_b[p][1], y_dn)

    def send_c(p):
        for way in range(2):
            n = 1 + way
            arrived(cx.at[p, n], core_sum[p][n])
            rc_send[p, way, 1 - way] = (pa[p, n, 1 - way] + cx[p, n, 1 - way].astype(F32)).astype(BF)
            arrived(rb.at[p, way], sem_b[p][way])
            rc_send[p, way, way] = (
                pa[p, n, way] + cx[p, n, way].astype(F32) + rb[p, way].astype(F32)).astype(BF)
            push(rc_send.at[p, way], rc.at[p, way], sem_c[p][way], y_up if way == 0 else y_dn)

    def send_g(p):
        arrived(cx.at[p, 3], core_sum[p][3])
        total = pa[p, 3] + cx[p, 3].astype(F32)
        for way in range(2):
            arrived(rc.at[p, way], sem_c[p][way])
            total = total + rc[p, way].astype(F32)
        fg[:, :, lanes_of(parts[p])] = total.astype(BF)
        for i in range(2):
            zk = parts[p] * 2 + i
            src = fg.at[:, :, pl.ds(mm(zk * 128), 128)]
            dst = gr.at[:, pl.ds(mm(z * EIGHTH, 16), EIGHTH), :]
            if p < 3:
                push(src, dst, g_recv + z, dev(x, c, y, zk))
        if p == 3:
            zk = z + 1 - 2 * (z % 2)
            push(fg.at[:, :, pl.ds(mm(zk * 128), 128)],
                 gr.at[:, pl.ds(mm(z * EIGHTH, 16), EIGHTH), :], g_recv + z, dev(x, c, y, zk))
            own = pltpu.make_async_copy(fg.at[:, :, pl.ds(mm(z * 128), 128)],
                                        gr.at[:, pl.ds(mm(z * EIGHTH, 16), EIGHTH), :], load_sems.at[5])
            own.start()
            own.wait()

    gradient(0)
    gradient(1)
    send_b(0)
    gradient(2)
    send_b(1)
    send_c(0)
    gradient(3)
    send_b(2)
    send_c(1)
    send_g(0)
    send_b(3)
    send_c(2)
    send_g(1)
    send_c(3)

    for k in range(NZ):
        zk = (z + k) % NZ
        for e in range(NC):
            if k == 0 and e == 0:
                continue
            ck = (c + e) % NC
            arrived(hr.at[pl.ds(mm(zk * EIGHTH, 16), EIGHTH), pl.ds(mm(ck * BLK), BLK)],
                    hid_recv + zk * NC + ck)
    hid[...] = hr[...].astype(F32).T.astype(BF)

    send_g(2)
    send_g(3)
    for k in range(1, NZ):
        zk = (z + k) % NZ
        arrived(gr.at[:, pl.ds(mm(zk * EIGHTH, 16), EIGHTH), :], g_recv + zk)
    both = jnp.concatenate([gr[0], gr[1]], axis=1)
    wg[...] = dot_nt(interleave_matrix(), both).astype(BF)

    def drain(k, _):
        own_copy((t + k) % NT).wait_send()
        return 0

    lax.fori_loop(1, NT, drain, 0)
    for copy in started:
        copy.wait_send()
    assert ssem.n <= send_sems.shape[0] and rsem.n <= recv_sems.shape[0], (ssem.n, rsem.n)


def per_device(activations, cotangent, old_gate_up, kept_index, new_slot):
    any_ = pl.BlockSpec(memory_space=pl.ANY)
    vmem = pl.BlockSpec(memory_space=pltpu.VMEM)
    V = pltpu.VMEM
    student, hidden, grad = pl.pallas_call(
        kernel,
        out_shape=(
            jax.ShapeDtypeStruct((256, OWN), BF),
            jax.ShapeDtypeStruct((256, OWN), BF),
            jax.ShapeDtypeStruct((256, OWN), BF),
        ),
        in_specs=[any_] * 5,
        out_specs=(vmem, vmem, vmem),
        scratch_shapes=[
            V((BLK, D), BF),
            V((256, OWN), BF),
            V((256, ROWS), BF),
            V((1, KEEP), jnp.int32),
            V((1, KEEP), jnp.int32),
            V((NZ, BLK, D), BF),
            V((8, KEEP), jnp.int32),
            V((KB * 16, 128), BF),
            V((KB * 16, 128), F32),
            V((CAP, ROWS), BF),
            V((NT, CAP, 256), BF),
            V((PLACES, 256), BF),
            V((OWN, 256), BF),
            V((2, OWN, 128), BF),
            V((NC, NY, 2, EIGHTH, CHUNK), BF),
            V((OWN, 256), BF),
            V((NC, EIGHTH, TOK), BF),
            V((NC, EIGHTH, TOK), BF),
            V((OWN, 256), BF),
            V((NC, 2 * EIGHTH, TOK), BF),
            V((4, NY, 2, EIGHTH, 256), BF),
            V((4, NY, 2, EIGHTH, 256), BF),
            V((4, NY, 2, EIGHTH, 256), F32),
            V((4, 2, EIGHTH, 256), BF),
            V((4, 2, EIGHTH, 256), BF),
            V((4, 2, 2, EIGHTH, 256), BF),
            V((4, 2, 2, EIGHTH, 256), BF),
            V((2, EIGHTH, CHUNK), BF),
            V((2, OWN, 128), BF),
            pltpu.SemaphoreType.DMA((6,)),
            pltpu.SemaphoreType.DMA((224,)),
            pltpu.SemaphoreType.DMA((224,)),
        ],
        compiler_params=pltpu.CompilerParams(
            collective_id=0, has_side_effects=True, vmem_limit_bytes=60 * 1024 * 1024),
        cost_estimate=pl.CostEstimate(flops=12_000_000_000, bytes_accessed=8_000_000, transcendentals=1_000_000),
        name="student_projection",
    )(activations, cotangent, old_gate_up.reshape(256, ROWS),
      kept_index.reshape(1, KEEP), new_slot.reshape(1, KEEP))
    return student.reshape(128, 2, OWN), hidden, grad.reshape(128, 2, OWN)


def solution(mesh):
    placed = (P("dp", None), P("dp", "tensor"), P("dp", None, "tensor"), P(), P())
    return jax.shard_map(
        per_device,
        mesh=mesh,
        in_specs=placed,
        out_specs=(P("dp", None, "tensor"), P("dp", "tensor"), P("dp", None, "tensor")),
        check_vma=False,
    )
```

```python
import jax
import jax.numpy as jnp
from jax import lax
from jax.experimental import pallas as pl
from jax.experimental.pallas import tpu as pltpu
from jax.sharding import PartitionSpec as P

MESH = pl.DeviceIdType.MESH
NZ, NY, NX, NC = 8, 4, 4, 2
NT = NX * NC
D = 4096
KEEP = 7168
OWN = 896
ROWS = 3584
CAP = 176
PLACES = NT * CAP
EIGHTH = OWN // NZ
BLK = 128
TOK = NZ * BLK
CHUNK = D // NY
DIRECT = 1024
SHARE = (D - DIRECT) // NX
HALF = BLK // 2
KB = KEEP // 128
F32 = jnp.float32
BF = jnp.bfloat16


def iota(shape, dim):
    return lax.broadcasted_iota(jnp.int32, shape, dim)


def dot(a, b):
    return lax.dot_general(a, b, (((1,), (0,)), ((), ())), preferred_element_type=F32)


def dot_nt(a, b):
    return lax.dot_general(a, b, (((1,), (1,)), ((), ())), preferred_element_type=F32)


def onehot(cond):
    return jnp.where(cond, 1.0, 0.0).astype(BF)


def interleave_matrix():
    a = iota((256, 256), 0)
    return onehot(iota((256, 256), 1) == (a & 1) * 128 + (a >> 1))


def mm(i, m=128):
    return pl.multiple_of(i, m)


class Sems:
    def __init__(self, ref):
        self.ref, self.n = ref, 0

    def take(self, count=1):
        first = self.n
        self.n += count
        return first


def finish(stn, hr, gr, stu, hid, wg, stn_v, hr_v, gr_v, stu_v, hid_v, wg_v, sems):
    loads = [pltpu.make_async_copy(a, b, sems.at[i])
             for i, (a, b) in enumerate(((stn, stn_v), (hr, hr_v), (gr, gr_v)))]
    stores = [pltpu.make_async_copy(a, b, sems.at[i + 3])
              for i, (a, b) in enumerate(((stu_v, stu), (hid_v, hid), (wg_v, wg)))]
    for load in loads:
        load.start()
    loads[0].wait()
    stu_v[...] = stn_v[...].astype(F32).T.astype(BF).reshape(128, 2, OWN)
    stores[0].start()
    loads[1].wait()
    hid_v[...] = hr_v[...].astype(F32).T.astype(BF)
    stores[1].start()
    loads[2].wait()
    both = jnp.concatenate([gr_v[0], gr_v[1]], axis=1)
    wg_v[...] = dot_nt(interleave_matrix(), both).astype(BF).reshape(128, 2, OWN)
    stores[2].start()
    for store in stores:
        store.wait()


def kernel(act, cot, old, kept, slot, stn, hr, gr,
           a_in, c_in, o_in, o_two, krow, srow, ab, idx, ohs, inc, pb, rts, rr, st2, wt, ct, cb,
           hs, gu, dg, cs, cx, pa, rb_send, rb, rc_send, rc, fg,
           load_sems, send_sems, recv_sems):
    dp = lax.axis_index("dp")
    t = lax.axis_index("tensor")
    z, y = dp // NY, dp % NY
    x, c = t // NC, t % NC

    def dev(x_, c_, y_, z_):
        return (z_ * NY + y_, x_ * NC + c_)

    sib = dev(x, 1 - c, y, z)
    z_up, z_dn = dev(x, c, y, (z + 1) % NZ), dev(x, c, y, (z + NZ - 1) % NZ)
    y_up, y_dn = dev(x, c, (y + 1) % NY, z), dev(x, c, (y + NY - 1) % NY, z)
    x_up, x_dn = dev((x + 1) % NX, c, y, z), dev((x + NX - 1) % NX, c, y, z)

    ssem, rsem = Sems(send_sems), Sems(recv_sems)
    started = []

    def push(src, dst, recv, device):
        copy = pltpu.make_async_remote_copy(
            src_ref=src, dst_ref=dst, send_sem=send_sems.at[ssem.take()],
            recv_sem=recv_sems.at[recv], device_id=device, device_id_type=MESH)
        copy.start()
        started.append(copy)

    def arrived(dst, recv):
        pltpu.make_async_remote_copy(
            src_ref=dst, dst_ref=dst, send_sem=send_sems.at[0],
            recv_sem=recv_sems.at[recv], device_id=sib, device_id_type=MESH).wait_recv()

    partners = []
    for k in range(1, NT):
        tk = (t + k) % NT
        partners.append((dp, tk))
    for k in range(1, NZ):
        zk = (z + k) % NZ
        partners.append(dev(x, c, y, zk))
        partners.append(dev(x, 1 - c, y, zk))
    partners.append(y_up)
    partners.append(y_dn)
    barrier = pltpu.get_barrier_semaphore()
    for p in partners:
        pl.semaphore_signal(barrier, inc=1, device_id=p, device_id_type=MESH)

    loads = [
        pltpu.make_async_copy(act.at[pl.ds(mm(c * BLK), BLK), :], a_in, load_sems.at[0]),
        pltpu.make_async_copy(cot, c_in, load_sems.at[1]),
        pltpu.make_async_copy(kept, krow, load_sems.at[2]),
        pltpu.make_async_copy(slot, srow, load_sems.at[3]),
        pltpu.make_async_copy(old, o_in, load_sems.at[4]),
    ]
    for load in loads:
        load.start()

    loads[0].wait()
    for yy in range(NY):
        for zz in range(NZ):
            ab[z, :, yy * CHUNK + zz * 128:yy * CHUNK + (zz + 1) * 128] = (
                a_in[:, (zz * NY + yy) * 128:(zz * NY + yy + 1) * 128])

    def share(xx):
        return pl.ds(mm(DIRECT + xx % NX * SHARE), SHARE)

    regions = [share(x), pl.ds(0, DIRECT)]
    ring_recv = [[[rsem.take(), rsem.take()] for _ in range(2)] for _ in range(4)]
    hand_recv = [[rsem.take(4), rsem.take(4)] for _ in range(4)]

    def ring_block(step, way):
        return (z + NZ - step) % NZ if way == 0 else (z + step) % NZ

    def ring_rows(step, way):
        if step < 4:
            return pl.ds(0, BLK)
        return pl.ds(0, HALF) if way == 0 else pl.ds(HALF, HALF)

    def ring_send(step, r):
        for way in range(2):
            piece = ab.at[ring_block(step - 1, way), ring_rows(step, way), regions[r]]
            push(piece, piece, ring_recv[step - 1][way][r], z_up if way == 0 else z_dn)

    def ring_wait(step, r):
        for way in range(2):
            arrived(ab.at[ring_block(step, way), ring_rows(step, way), regions[r]],
                    ring_recv[step - 1][way][r])

    def hand_blocks(step):
        return [(ring_block(step, way), hand_recv[step - 1][way]) for way in range(2 if step < 4 else 1)]

    def hand_on(step):
        for block, sem in hand_blocks(step):
            piece = ab.at[block, :, share(x)]
            push(piece, piece, sem, x_up)
            push(piece, piece, sem + 1, x_dn)

    def relay(step):
        for block, sem in hand_blocks(step):
            arrived(ab.at[block, :, share(x + 3)], sem)
            piece = ab.at[block, pl.ds(0, HALF), share(x + 3)]
            push(piece, piece, sem + 2, x_up)
            arrived(ab.at[block, :, share(x + 1)], sem + 1)
            piece = ab.at[block, pl.ds(HALF, HALF), share(x + 1)]
            push(piece, piece, sem + 3, x_dn)

    def handed(step):
        for block, sem in hand_blocks(step):
            arrived(ab.at[block, pl.ds(0, HALF), share(x + 2)], sem + 2)
            arrived(ab.at[block, pl.ds(HALF, HALF), share(x + 2)], sem + 3)

    def ring(step, r):
        ring_wait(step, r)
        if step < 4:
            ring_send(step + 1, r)
        if r == 0:
            hand_on(step)

    loads[1].wait()
    ct[...] = c_in[...].astype(F32).T.astype(BF)
    cot_recv = rsem.take(NZ * NC)
    cot_slot = cot_recv + z * NC + c

    def cot_push(k, e):
        zk, ck = (z + k) % NZ, (c + e) % NC
        src = ct.at[pl.ds(mm(zk * EIGHTH, 16), EIGHTH), pl.ds(mm(ck * BLK), BLK)]
        dst = cb.at[c, :, pl.ds(mm(z * BLK), BLK)]
        if k == 0 and e == 0:
            own = pltpu.make_async_copy(src, dst, load_sems.at[5])
            own.start()
            own.wait()
        else:
            push(src, dst, cot_slot, dev(x, ck, y, zk))

    def both_ways(k):
        return (k, NZ - k) if k < 4 else (4,)

    def cot_out(distance):
        for k in both_ways(distance):
            for e in range(NC):
                cot_push(k, e)

    loads[2].wait()
    loads[3].wait()
    kv, sv = krow[...], srow[...]
    o, j = jnp.zeros_like(kv), jnp.zeros_like(sv)
    for i in range(1, NT):
        o = o + jnp.where(kv >= ROWS * i, 1, 0)
        j = j + jnp.where(sv >= OWN * i, 1, 0)
    idx[0:1, :] = jnp.where(o == t, j, 99)
    idx[1:2, :] = jnp.where(j == t, o + 8, 99)
    row16 = iota((16, 128), 0)
    for b in range(KB):
        lanes = slice(b * 128, (b + 1) * 128)
        key = jnp.where(row16 < 8, jnp.broadcast_to(idx[0:1, lanes], (16, 128)),
                        jnp.broadcast_to(idx[1:2, lanes], (16, 128)))
        ohs[b * 16:(b + 1) * 16, :] = onehot(key == row16)
    upto = onehot(iota((128, 128), 0) <= iota((128, 128), 1))
    inc[...] = dot(ohs[...], upto)
    run = jnp.zeros((16, 1), F32)
    for b in range(KB):
        lanes = slice(b * 128, (b + 1) * 128)
        here = inc[b * 16:(b + 1) * 16, :]
        rank = ohs[b * 16:(b + 1) * 16, :].astype(F32) * (here + run)
        rank_s = jnp.sum(rank[0:8], axis=0, keepdims=True).astype(jnp.int32)
        rank_r = jnp.sum(rank[8:16], axis=0, keepdims=True).astype(jnp.int32)
        dest, source = idx[0:1, lanes], idx[1:2, lanes]
        idx[2:3, lanes] = jnp.where(dest < 99, dest * CAP + rank_s, 0)
        idx[3:4, lanes] = jnp.where(source < 99, (source - 8) * CAP + rank_r, 0)
        run = run + here[:, 127:128]
    idx[4:5, :] = kv - t * ROWS
    idx[5:6, :] = sv - t * OWN

    def scatter(step, carry):
        by_neuron, by_slot = carry
        lanes = pl.ds(mm(step * OWN), OWN)
        vs, vr, ln, ls = (idx[i:i + 1, lanes] for i in (2, 3, 4, 5))
        high = iota((32, OWN), 0) == (ln >> 7)
        values = jnp.concatenate([
            jnp.where(high, vs >> 7, 0), jnp.where(high, vs & 127, 0)], axis=0)
        low = onehot(iota((128, OWN), 0) == (ln & 127))
        by_neuron = by_neuron + dot_nt(values.astype(F32).astype(BF), low)
        high = iota((8, OWN), 0) == (ls >> 7)
        values = jnp.concatenate([
            jnp.where(high, vr >> 7, 0), jnp.where(high, vr & 127, 0)], axis=0)
        low = onehot(iota((128, OWN), 0) == (ls & 127))
        by_slot = by_slot + dot_nt(low, values.astype(F32).astype(BF))
        return by_neuron, by_slot

    by_neuron, by_slot = lax.fori_loop(
        0, KEEP // OWN, scatter, (jnp.zeros((64, 128), F32), jnp.zeros((128, 16), F32)))
    place_s = (by_neuron[0:32] * 128.0 + by_neuron[32:64]).astype(jnp.int32)
    place_r = (by_slot[:, 0:8] * 128.0 + by_slot[:, 8:16]).astype(jnp.int32)

    loads[4].wait()
    o_two[...] = o_in[...].reshape(256, ROWS)

    pl.semaphore_wait(barrier, len(partners))
    ring_send(1, 0)
    ring_send(1, 1)
    own_recv = rsem.take(NT)
    own_send = ssem.take(NT)

    def own_copy(to):
        return pltpu.make_async_remote_copy(
            src_ref=rts.at[to], dst_ref=rr.at[pl.ds(mm(t * CAP, 16), CAP), :],
            send_sem=send_sems.at[own_send + to], recv_sem=recv_sems.at[own_recv + t],
            device_id=(dp, to), device_id_type=MESH)

    def select(k, _):
        to = (t + k) % NT
        row = iota((CAP, 128), 0) + (to * CAP + 1)
        for h in range(ROWS // 128):
            pb[:, h * 128:(h + 1) * 128] = onehot(place_s[h:h + 1, :] == row)
        rts[to] = dot_nt(pb[...], o_two[...]).astype(BF)
        return 0

    lax.fori_loop(0, NT, select, 0)

    def own_start(k, _):
        own_copy((t + k) % NT).start()
        return 0

    lax.fori_loop(1, NT, own_start, 0)
    rr[pl.ds(mm(t * CAP, 16), CAP), :] = rts[t]

    cot_out(4)
    cot_push(0, 1)
    ring(1, 0)
    for k in range(1, NT):
        frm = (t + k) % NT
        arrived(rr.at[pl.ds(mm(frm * CAP, 16), CAP), :], own_recv + frm)
    pi = interleave_matrix()
    got = rr[...]
    for h in range(OWN // 128):
        q = onehot(iota((128, PLACES), 1) + 1 == place_r[:, h:h + 1])
        mine = dot(q, got).astype(BF)
        stn[h * 128:(h + 1) * 128, :] = mine
        split = dot(mine, pi).astype(BF)
        st2[0, h * 128:(h + 1) * 128, :] = split[:, 0:128]
        st2[1, h * 128:(h + 1) * 128, :] = split[:, 128:256]

    w_recv = rsem.take(NZ)

    def eighth(k):
        zk = (z + k) % NZ
        return (st2.at[:, pl.ds(mm(zk * EIGHTH, 16), EIGHTH), :],
                wt.at[c, y, :, :, pl.ds(mm(z * 128), 128)], dev(x, c, y, zk))

    own = pltpu.make_async_copy(*eighth(0)[:2], load_sems.at[5])
    own.start()
    own.wait()

    def w_out(distance):
        for k in both_ways(distance):
            src, dst, to = eighth(k)
            push(src, dst, w_recv + z, to)

    y1, y3, y2 = (y + 1) % NY, (y + 3) % NY, (y + 2) % NY
    pairs = [(z // 2 + k) % (NZ // 2) for k in (0, 1, 3, 2)]
    wy = [rsem.take(4) for _ in pairs]
    core_recv = rsem.take(NY * len(pairs))

    def w_part(cc, yy, pair):
        return wt.at[cc, yy, :, :, pl.ds(mm(pair * 256, 256), 256)]

    def w_half(yy, g, pair):
        return wt.at[c, yy, g, :, pl.ds(mm(pair * 256, 256), 256)]

    def to_core(yy, pair):
        push(w_part(c, yy, pair), w_part(c, yy, pair), core_recv + pair * NY + yy, sib)

    def w_round(n):
        pair = pairs[n]
        for zk in ([z + 1 - 2 * (z % 2)] if n == 0 else [pair * 2, pair * 2 + 1]):
            arrived(wt.at[c, y, :, :, pl.ds(mm(zk * 128), 128)], w_recv + zk)
        push(w_part(c, y, pair), w_part(c, y, pair), wy[n], y_up)
        push(w_part(c, y, pair), w_part(c, y, pair), wy[n] + 1, y_dn)
        to_core(y, pair)

    def w_relay(n):
        pair = pairs[n]
        arrived(w_part(c, y3, pair), wy[n])
        push(w_half(y3, 0, pair), w_half(y3, 0, pair), wy[n] + 2, y_up)
        arrived(w_part(c, y1, pair), wy[n] + 1)
        push(w_half(y1, 1, pair), w_half(y1, 1, pair), wy[n] + 3, y_dn)
        to_core(y3, pair)
        to_core(y1, pair)

    def w_last(n):
        pair = pairs[n]
        arrived(w_half(y2, 0, pair), wy[n] + 2)
        arrived(w_half(y2, 1, pair), wy[n] + 3)
        to_core(y2, pair)

    def w_from_core():
        for pair in pairs:
            for yy in (y, y3, y1, y2):
                arrived(w_part(1 - c, yy, pair), core_recv + pair * NY + yy)

    hid_recv = rsem.take(NZ * NC)

    def forward(blocks):
        tokens = jnp.concatenate([ab[b] for b in blocks], axis=0)
        total = jnp.zeros((448, 256), F32)
        for yy in range(NY):
            total = total + dot_nt(wt[:, yy].reshape(448, CHUNK),
                                   tokens[:, yy * CHUNK:(yy + 1) * CHUNK])
        for cc in range(NC):
            for i, b in enumerate(blocks):
                lanes = pl.ds(mm(b * BLK), BLK)
                gate = total[cc * 224:cc * 224 + 112, i * BLK:(i + 1) * BLK]
                up = total[cc * 224 + 112:cc * 224 + 224, i * BLK:(i + 1) * BLK]
                gu[cc, 0, :, lanes] = gate
                gu[cc, 1, :, lanes] = up
                hs[cc, :, lanes] = (gate * jax.nn.sigmoid(gate) * up).astype(BF)

    def backward(blocks):
        for cc in range(NC):
            for b in blocks:
                lanes = pl.ds(mm(b * BLK), BLK)
                gate, up = gu[cc, 0, :, lanes], gu[cc, 1, :, lanes]
                sig = jax.nn.sigmoid(gate)
                silu = gate * sig
                incoming = cb[cc, :, lanes].astype(F32)
                dg[cc, 0:112, lanes] = (incoming * up * sig * (1.0 + gate * (1.0 - sig))).astype(BF)
                dg[cc, 112:224, lanes] = (incoming * silu).astype(BF)

    def hidden_out(k):
        zk = (z + k) % NZ
        for e in range(NC):
            ck = (c + e) % NC
            src = hs.at[ck, :, pl.ds(mm(zk * BLK), BLK)]
            dst = hr.at[pl.ds(mm(z * EIGHTH, 16), EIGHTH), pl.ds(mm(c * BLK), BLK)]
            if k == 0 and e == 0:
                own = pltpu.make_async_copy(src, dst, load_sems.at[5])
                own.start()
                own.wait()
            else:
                push(src, dst, hid_recv + z * NC + c, dev(x, ck, y, zk))

    def blocks_of(step):
        return [ring_block(step, 0), ring_block(step, 1) if step < 4 else z]

    def cot_in():
        cot_push(0, 0)
        for k in range(NZ):
            zk = (z + k) % NZ
            for e in range(NC):
                if k == 0 and e == 0:
                    continue
                ck = (c + e) % NC
                arrived(cb.at[ck, :, pl.ds(mm(zk * BLK), BLK)], cot_recv + zk * NC + ck)

    w_out(3)
    w_out(1)
    ring(2, 0)
    w_out(2)
    w_round(2)
    w_round(0)
    relay(1)
    ring(1, 1)
    w_out(4)
    ring(3, 0)
    w_relay(0)
    ring(4, 0)
    ring(2, 1)
    w_relay(2)
    cot_out(1)
    relay(2)
    cot_out(2)
    w_last(0)
    w_round(3)
    w_last(2)
    w_round(1)
    w_relay(3)
    w_relay(1)
    cot_out(3)
    relay(3)
    w_last(3)
    handed(2)
    handed(1)
    relay(4)
    ring(3, 1)
    w_last(1)
    w_from_core()
    forward(blocks_of(2))
    handed(3)
    forward(blocks_of(1))
    forward(blocks_of(3))
    cot_in()
    backward(blocks_of(2))
    backward(blocks_of(1))
    backward(blocks_of(3))
    handed(4)
    ring_wait(4, 1)
    forward(blocks_of(4))
    backward(blocks_of(4))
    order = [y2, y1, y3, y]
    parts = [(z // 2 + k) % (NZ // 2) for k in (2, 1, 3, 0)]
    core_sum = [[rsem.take() for _ in order] for _ in parts]
    sem_b = [[rsem.take(), rsem.take()] for _ in parts]
    sem_c = [[rsem.take(), rsem.take()] for _ in parts]
    g_recv = rsem.take(NZ)

    def lanes_of(pair):
        return pl.ds(mm(pair * 256, 256), 256)

    def gradient(p, n):
        yy = order[n]
        width = ab[:, :, pl.ds(mm(yy * CHUNK + parts[p] * 256, 256), 256)].reshape(TOK, 256)
        cs[p, n] = dot(dg[1 - c], width).astype(BF).reshape(2, EIGHTH, 256)
        push(cs.at[p, n], cx.at[p, n], core_sum[p][n], sib)
        pa[p, n] = dot(dg[c], width).reshape(2, EIGHTH, 256)

    def send_b(p):
        arrived(cx.at[p, 0], core_sum[p][0])
        rb_send[p] = (pa[p, 0] + cx[p, 0].astype(F32)).astype(BF)
        push(rb_send.at[p, 0], rb.at[p, 0], sem_b[p][0], y_up)
        push(rb_send.at[p, 1], rb.at[p, 1], sem_b[p][1], y_dn)

    def send_c(p):
        for way in range(2):
            n = 1 + way
            arrived(cx.at[p, n], core_sum[p][n])
            rc_send[p, way, 1 - way] = (pa[p, n, 1 - way] + cx[p, n, 1 - way].astype(F32)).astype(BF)
            arrived(rb.at[p, way], sem_b[p][way])
            rc_send[p, way, way] = (
                pa[p, n, way] + cx[p, n, way].astype(F32) + rb[p, way].astype(F32)).astype(BF)
            push(rc_send.at[p, way], rc.at[p, way], sem_c[p][way], y_up if way == 0 else y_dn)

    def send_g(p):
        arrived(cx.at[p, 3], core_sum[p][3])
        total = pa[p, 3] + cx[p, 3].astype(F32)
        for way in range(2):
            arrived(rc.at[p, way], sem_c[p][way])
            total = total + rc[p, way].astype(F32)
        fg[:, :, lanes_of(parts[p])] = total.astype(BF)
        for i in range(2):
            zk = parts[p] * 2 + i
            src = fg.at[:, :, pl.ds(mm(zk * 128), 128)]
            dst = gr.at[:, pl.ds(mm(z * EIGHTH, 16), EIGHTH), :]
            if p < 3:
                push(src, dst, g_recv + z, dev(x, c, y, zk))
        if p == 3:
            zk = z + 1 - 2 * (z % 2)
            push(fg.at[:, :, pl.ds(mm(zk * 128), 128)],
                 gr.at[:, pl.ds(mm(z * EIGHTH, 16), EIGHTH), :], g_recv + z, dev(x, c, y, zk))
            own = pltpu.make_async_copy(fg.at[:, :, pl.ds(mm(z * 128), 128)],
                                        gr.at[:, pl.ds(mm(z * EIGHTH, 16), EIGHTH), :], load_sems.at[5])
            own.start()
            own.wait()

    gradient(0, 0)
    gradient(1, 0)
    gradient(2, 0)
    send_b(0)
    gradient(3, 0)
    send_b(1)
    send_b(2)
    send_b(3)
    for k in (4, 3, 5, 2, 6, 1, 7, 0):
        hidden_out(k)
    for p in range(4):
        gradient(p, 1)
        gradient(p, 2)
    for p in range(4):
        send_c(p)
        gradient(p, 3)
    send_g(0)
    send_g(1)

    for k in range(NZ):
        zk = (z + k) % NZ
        for e in range(NC):
            if k == 0 and e == 0:
                continue
            ck = (c + e) % NC
            arrived(hr.at[pl.ds(mm(zk * EIGHTH, 16), EIGHTH), pl.ds(mm(ck * BLK), BLK)],
                    hid_recv + zk * NC + ck)
    send_g(2)
    send_g(3)
    for k in range(1, NZ):
        zk = (z + k) % NZ
        arrived(gr.at[:, pl.ds(mm(zk * EIGHTH, 16), EIGHTH), :], g_recv + zk)
    def drain(k, _):
        own_copy((t + k) % NT).wait_send()
        return 0

    lax.fori_loop(1, NT, drain, 0)
    for copy in started:
        copy.wait_send()
    assert ssem.n <= send_sems.shape[0] and rsem.n <= recv_sems.shape[0], (ssem.n, rsem.n)


def per_device(activations, cotangent, old_gate_up, kept_index, new_slot):
    any_ = pl.BlockSpec(memory_space=pl.ANY)
    vmem = pl.BlockSpec(memory_space=pltpu.VMEM)
    V = pltpu.VMEM
    raw = pl.pallas_call(
        kernel,
        out_shape=(
            jax.ShapeDtypeStruct((OWN, 256), BF),
            jax.ShapeDtypeStruct((OWN, 256), BF),
            jax.ShapeDtypeStruct((2, OWN, 128), BF),
        ),
        in_specs=[any_] * 5,
        out_specs=(vmem, vmem, vmem),
        scratch_shapes=[
            V((BLK, D), BF),
            V((256, OWN), BF),
            V((128, 2, ROWS), BF),
            V((256, ROWS), BF),
            V((1, KEEP), jnp.int32),
            V((1, KEEP), jnp.int32),
            V((NZ, BLK, D), BF),
            V((8, KEEP), jnp.int32),
            V((KB * 16, 128), BF),
            V((KB * 16, 128), F32),
            V((CAP, ROWS), BF),
            V((NT, CAP, 256), BF),
            V((PLACES, 256), BF),
            V((2, OWN, 128), BF),
            V((NC, NY, 2, EIGHTH, CHUNK), BF),
            V((OWN, 256), BF),
            V((NC, EIGHTH, TOK), BF),
            V((NC, EIGHTH, TOK), BF),
            V((NC, 2, EIGHTH, TOK), F32),
            V((NC, 2 * EIGHTH, TOK), BF),
            V((4, NY, 2, EIGHTH, 256), BF),
            V((4, NY, 2, EIGHTH, 256), BF),
            V((4, NY, 2, EIGHTH, 256), F32),
            V((4, 2, EIGHTH, 256), BF),
            V((4, 2, EIGHTH, 256), BF),
            V((4, 2, 2, EIGHTH, 256), BF),
            V((4, 2, 2, EIGHTH, 256), BF),
            V((2, EIGHTH, CHUNK), BF),
            pltpu.SemaphoreType.DMA((6,)),
            pltpu.SemaphoreType.DMA((224,)),
            pltpu.SemaphoreType.DMA((224,)),
        ],
        compiler_params=pltpu.CompilerParams(
            collective_id=0, has_side_effects=True, vmem_limit_bytes=60 * 1024 * 1024),
        cost_estimate=pl.CostEstimate(flops=12_000_000_000, bytes_accessed=8_000_000, transcendentals=1_000_000),
        name="student_projection",
    )(activations, cotangent, old_gate_up,
      kept_index.reshape(1, KEEP), new_slot.reshape(1, KEEP))
    return pl.pallas_call(
        finish,
        out_shape=(
            jax.ShapeDtypeStruct((128, 2, OWN), BF),
            jax.ShapeDtypeStruct((256, OWN), BF),
            jax.ShapeDtypeStruct((128, 2, OWN), BF),
        ),
        in_specs=[any_] * 3,
        out_specs=(any_,) * 3,
        scratch_shapes=[
            V((OWN, 256), BF), V((OWN, 256), BF), V((2, OWN, 128), BF),
            V((128, 2, OWN), BF), V((256, OWN), BF), V((128, 2, OWN), BF),
            pltpu.SemaphoreType.DMA((6,)),
        ],
        compiler_params=pltpu.CompilerParams(vmem_limit_bytes=60 * 1024 * 1024),
        name="finish",
    )(*raw)


def solution(mesh):
    placed = (P("dp", None), P("dp", "tensor"), P("dp", None, "tensor"), P(), P())
    return jax.shard_map(
        per_device,
        mesh=mesh,
        in_specs=placed,
        out_specs=(P("dp", None, "tensor"), P("dp", "tensor"), P("dp", None, "tensor")),
        check_vma=False,
    )
```

```python
import jax
import jax.numpy as jnp
from jax import lax
from jax.experimental import pallas as pl
from jax.experimental.pallas import tpu as pltpu
from jax.sharding import PartitionSpec as P

MESH = pl.DeviceIdType.MESH
NZ, NY, NX, NC = 8, 4, 4, 2
NT = NX * NC
D = 4096
KEEP = 7168
OWN = 896
ROWS = 3584
CAP = 176
PLACES = NT * CAP
EIGHTH = OWN // NZ
BLK = 128
TOK = NZ * BLK
CHUNK = D // NY
DIRECT = 1024
SHARE = (D - DIRECT) // NX
HALF = BLK // 2
KB = KEEP // 128
F32 = jnp.float32
BF = jnp.bfloat16


def iota(shape, dim):
    return lax.broadcasted_iota(jnp.int32, shape, dim)


def dot(a, b):
    return lax.dot_general(a, b, (((1,), (0,)), ((), ())), preferred_element_type=F32)


def dot_nt(a, b):
    return lax.dot_general(a, b, (((1,), (1,)), ((), ())), preferred_element_type=F32)


def onehot(cond):
    return jnp.where(cond, 1.0, 0.0).astype(BF)


def interleave_matrix():
    a = iota((256, 256), 0)
    return onehot(iota((256, 256), 1) == (a & 1) * 128 + (a >> 1))


def mm(i, m=128):
    return pl.multiple_of(i, m)


class Sems:
    def __init__(self, ref):
        self.ref, self.n = ref, 0

    def take(self, count=1):
        first = self.n
        self.n += count
        return first


def finish(stn, hr, gr, stu, hid, wg, stn_v, hr_v, gr_v, stu_v, hid_v, wg_v, sems):
    loads = [pltpu.make_async_copy(a, b, sems.at[i])
             for i, (a, b) in enumerate(((stn, stn_v), (hr, hr_v), (gr, gr_v)))]
    stores = [pltpu.make_async_copy(a, b, sems.at[i + 3])
              for i, (a, b) in enumerate(((stu_v, stu), (hid_v, hid), (wg_v, wg)))]
    for load in loads:
        load.start()
    loads[0].wait()
    stu_v[...] = stn_v[...].astype(F32).T.astype(BF).reshape(128, 2, OWN)
    stores[0].start()
    loads[1].wait()
    hid_v[...] = hr_v[...].astype(F32).T.astype(BF)
    stores[1].start()
    loads[2].wait()
    both = jnp.concatenate([gr_v[0], gr_v[1]], axis=1)
    wg_v[...] = dot_nt(interleave_matrix(), both).astype(BF).reshape(128, 2, OWN)
    stores[2].start()
    for store in stores:
        store.wait()


def kernel(act, cot, old, kept, slot, stn, hr, gr,
           a_in, c_in, o_in, o_two, krow, srow, ab, idx, ohs, inc, pb, rts, rr, st2, wt, ct, cb,
           hs, gu, dg, cs, cx, pa, rb_send, rb, rc_send, rc, fg,
           load_sems, send_sems, recv_sems):
    dp = lax.axis_index("dp")
    t = lax.axis_index("tensor")
    z, y = dp // NY, dp % NY
    x, c = t // NC, t % NC

    def dev(x_, c_, y_, z_):
        return (z_ * NY + y_, x_ * NC + c_)

    sib = dev(x, 1 - c, y, z)
    z_up, z_dn = dev(x, c, y, (z + 1) % NZ), dev(x, c, y, (z + NZ - 1) % NZ)
    y_up, y_dn = dev(x, c, (y + 1) % NY, z), dev(x, c, (y + NY - 1) % NY, z)
    x_up, x_dn = dev((x + 1) % NX, c, y, z), dev((x + NX - 1) % NX, c, y, z)

    ssem, rsem = Sems(send_sems), Sems(recv_sems)
    started = []

    def push(src, dst, recv, device):
        copy = pltpu.make_async_remote_copy(
            src_ref=src, dst_ref=dst, send_sem=send_sems.at[ssem.take()],
            recv_sem=recv_sems.at[recv], device_id=device, device_id_type=MESH)
        copy.start()
        started.append(copy)

    def arrived(dst, recv):
        pltpu.make_async_remote_copy(
            src_ref=dst, dst_ref=dst, send_sem=send_sems.at[0],
            recv_sem=recv_sems.at[recv], device_id=sib, device_id_type=MESH).wait_recv()

    partners = []
    for k in range(1, NT):
        tk = (t + k) % NT
        partners.append((dp, tk))
    for k in range(1, NZ):
        zk = (z + k) % NZ
        partners.append(dev(x, c, y, zk))
        partners.append(dev(x, 1 - c, y, zk))
    partners.append(y_up)
    partners.append(y_dn)
    barrier = pltpu.get_barrier_semaphore()
    for p in partners:
        pl.semaphore_signal(barrier, inc=1, device_id=p, device_id_type=MESH)

    loads = [
        pltpu.make_async_copy(act.at[pl.ds(mm(c * BLK), BLK), :], a_in, load_sems.at[0]),
        pltpu.make_async_copy(cot, c_in, load_sems.at[1]),
        pltpu.make_async_copy(kept, krow, load_sems.at[2]),
        pltpu.make_async_copy(slot, srow, load_sems.at[3]),
        pltpu.make_async_copy(old, o_in, load_sems.at[4]),
    ]
    for load in loads:
        load.start()

    loads[0].wait()
    for yy in range(NY):
        for zz in range(NZ):
            ab[z, :, yy * CHUNK + zz * 128:yy * CHUNK + (zz + 1) * 128] = (
                a_in[:, (zz * NY + yy) * 128:(zz * NY + yy + 1) * 128])

    def share(xx):
        return pl.ds(mm(DIRECT + xx % NX * SHARE), SHARE)

    regions = [share(x), pl.ds(0, DIRECT)]
    ring_recv = [[[rsem.take(), rsem.take()] for _ in range(2)] for _ in range(4)]
    hand_recv = [[rsem.take(4), rsem.take(4)] for _ in range(4)]

    def ring_block(step, way):
        return (z + NZ - step) % NZ if way == 0 else (z + step) % NZ

    def ring_rows(step, way):
        if step < 4:
            return pl.ds(0, BLK)
        return pl.ds(0, HALF) if way == 0 else pl.ds(HALF, HALF)

    def ring_send(step, r):
        for way in range(2):
            piece = ab.at[ring_block(step - 1, way), ring_rows(step, way), regions[r]]
            push(piece, piece, ring_recv[step - 1][way][r], z_up if way == 0 else z_dn)

    def ring_wait(step, r):
        for way in range(2):
            arrived(ab.at[ring_block(step, way), ring_rows(step, way), regions[r]],
                    ring_recv[step - 1][way][r])

    def hand_blocks(step):
        return [(ring_block(step, way), hand_recv[step - 1][way]) for way in range(2 if step < 4 else 1)]

    def hand_on(step):
        for block, sem in hand_blocks(step):
            piece = ab.at[block, :, share(x)]
            push(piece, piece, sem, x_up)
            push(piece, piece, sem + 1, x_dn)

    def relay(step):
        for block, sem in hand_blocks(step):
            arrived(ab.at[block, :, share(x + 3)], sem)
            piece = ab.at[block, pl.ds(0, HALF), share(x + 3)]
            push(piece, piece, sem + 2, x_up)
            arrived(ab.at[block, :, share(x + 1)], sem + 1)
            piece = ab.at[block, pl.ds(HALF, HALF), share(x + 1)]
            push(piece, piece, sem + 3, x_dn)

    def handed(step):
        for block, sem in hand_blocks(step):
            arrived(ab.at[block, pl.ds(0, HALF), share(x + 2)], sem + 2)
            arrived(ab.at[block, pl.ds(HALF, HALF), share(x + 2)], sem + 3)

    def ring(step, r):
        ring_wait(step, r)
        if step < 4:
            ring_send(step + 1, r)
        if r == 0:
            hand_on(step)

    loads[1].wait()
    ct[...] = c_in[...].astype(F32).T.astype(BF)
    cot_recv = rsem.take(NZ * NC)
    cot_slot = cot_recv + z * NC + c

    def cot_push(k, e):
        zk, ck = (z + k) % NZ, (c + e) % NC
        src = ct.at[pl.ds(mm(zk * EIGHTH, 16), EIGHTH), pl.ds(mm(ck * BLK), BLK)]
        dst = cb.at[c, :, pl.ds(mm(z * BLK), BLK)]
        if k == 0 and e == 0:
            own = pltpu.make_async_copy(src, dst, load_sems.at[5])
            own.start()
            own.wait()
        else:
            push(src, dst, cot_slot, dev(x, ck, y, zk))

    def both_ways(k):
        return (k, NZ - k) if k < 4 else (4,)

    def cot_out(distance):
        for k in both_ways(distance):
            for e in range(NC):
                cot_push(k, e)

    loads[2].wait()
    loads[3].wait()
    kv, sv = krow[...], srow[...]
    o, j = jnp.zeros_like(kv), jnp.zeros_like(sv)
    for i in range(1, NT):
        o = o + jnp.where(kv >= ROWS * i, 1, 0)
        j = j + jnp.where(sv >= OWN * i, 1, 0)
    idx[0:1, :] = jnp.where(o == t, j, 99)
    idx[1:2, :] = jnp.where(j == t, o + 8, 99)
    row16 = iota((16, 128), 0)
    for b in range(KB):
        lanes = slice(b * 128, (b + 1) * 128)
        key = jnp.where(row16 < 8, jnp.broadcast_to(idx[0:1, lanes], (16, 128)),
                        jnp.broadcast_to(idx[1:2, lanes], (16, 128)))
        ohs[b * 16:(b + 1) * 16, :] = onehot(key == row16)
    upto = onehot(iota((128, 128), 0) <= iota((128, 128), 1))
    inc[...] = dot(ohs[...], upto)
    run = jnp.zeros((16, 1), F32)
    for b in range(KB):
        lanes = slice(b * 128, (b + 1) * 128)
        here = inc[b * 16:(b + 1) * 16, :]
        rank = ohs[b * 16:(b + 1) * 16, :].astype(F32) * (here + run)
        rank_s = jnp.sum(rank[0:8], axis=0, keepdims=True).astype(jnp.int32)
        rank_r = jnp.sum(rank[8:16], axis=0, keepdims=True).astype(jnp.int32)
        dest, source = idx[0:1, lanes], idx[1:2, lanes]
        idx[2:3, lanes] = jnp.where(dest < 99, dest * CAP + rank_s, 0)
        idx[3:4, lanes] = jnp.where(source < 99, (source - 8) * CAP + rank_r, 0)
        run = run + here[:, 127:128]
    idx[4:5, :] = kv - t * ROWS
    idx[5:6, :] = sv - t * OWN

    def scatter(step, carry):
        by_neuron, by_slot = carry
        lanes = pl.ds(mm(step * OWN), OWN)
        vs, vr, ln, ls = (idx[i:i + 1, lanes] for i in (2, 3, 4, 5))
        high = iota((32, OWN), 0) == (ln >> 7)
        values = jnp.concatenate([
            jnp.where(high, vs >> 7, 0), jnp.where(high, vs & 127, 0)], axis=0)
        low = onehot(iota((128, OWN), 0) == (ln & 127))
        by_neuron = by_neuron + dot_nt(values.astype(F32).astype(BF), low)
        high = iota((8, OWN), 0) == (ls >> 7)
        values = jnp.concatenate([
            jnp.where(high, vr >> 7, 0), jnp.where(high, vr & 127, 0)], axis=0)
        low = onehot(iota((128, OWN), 0) == (ls & 127))
        by_slot = by_slot + dot_nt(low, values.astype(F32).astype(BF))
        return by_neuron, by_slot

    by_neuron, by_slot = lax.fori_loop(
        0, KEEP // OWN, scatter, (jnp.zeros((64, 128), F32), jnp.zeros((128, 16), F32)))
    place_s = (by_neuron[0:32] * 128.0 + by_neuron[32:64]).astype(jnp.int32)
    place_r = (by_slot[:, 0:8] * 128.0 + by_slot[:, 8:16]).astype(jnp.int32)

    loads[4].wait()
    o_two[...] = o_in[...].reshape(256, ROWS)

    pl.semaphore_wait(barrier, len(partners))
    ring_send(1, 0)
    ring_send(1, 1)
    own_recv = rsem.take(NT)
    own_send = ssem.take(NT)

    def own_copy(to):
        return pltpu.make_async_remote_copy(
            src_ref=rts.at[to], dst_ref=rr.at[pl.ds(mm(t * CAP, 16), CAP), :],
            send_sem=send_sems.at[own_send + to], recv_sem=recv_sems.at[own_recv + t],
            device_id=(dp, to), device_id_type=MESH)

    def select(k, _):
        to = (t + k) % NT
        row = iota((CAP, 128), 0) + (to * CAP + 1)
        for h in range(ROWS // 128):
            pb[:, h * 128:(h + 1) * 128] = onehot(place_s[h:h + 1, :] == row)
        rts[to] = dot_nt(pb[...], o_two[...]).astype(BF)
        return 0

    lax.fori_loop(0, NT, select, 0)

    def own_start(k, _):
        own_copy((t + k) % NT).start()
        return 0

    lax.fori_loop(1, NT, own_start, 0)
    rr[pl.ds(mm(t * CAP, 16), CAP), :] = rts[t]

    cot_out(2)
    ring(1, 0)
    for k in range(1, NT):
        frm = (t + k) % NT
        arrived(rr.at[pl.ds(mm(frm * CAP, 16), CAP), :], own_recv + frm)
    pi = interleave_matrix()
    got = rr[...]
    for h in range(OWN // 128):
        q = onehot(iota((128, PLACES), 1) + 1 == place_r[:, h:h + 1])
        mine = dot(q, got).astype(BF)
        stn[h * 128:(h + 1) * 128, :] = mine
        split = dot(mine, pi).astype(BF)
        st2[0, h * 128:(h + 1) * 128, :] = split[:, 0:128]
        st2[1, h * 128:(h + 1) * 128, :] = split[:, 128:256]

    w_recv = rsem.take(NZ)

    def eighth(k):
        zk = (z + k) % NZ
        return (st2.at[:, pl.ds(mm(zk * EIGHTH, 16), EIGHTH), :],
                wt.at[c, y, :, :, pl.ds(mm(z * 128), 128)], dev(x, c, y, zk))

    own = pltpu.make_async_copy(*eighth(0)[:2], load_sems.at[5])
    own.start()
    own.wait()

    def w_out(distance):
        for k in both_ways(distance):
            src, dst, to = eighth(k)
            push(src, dst, w_recv + z, to)

    y1, y3, y2 = (y + 1) % NY, (y + 3) % NY, (y + 2) % NY
    pairs = [(z // 2 + k) % (NZ // 2) for k in (0, 1, 3, 2)]
    wy = [rsem.take(4) for _ in pairs]
    core_recv = rsem.take(NY * len(pairs))

    def w_part(cc, yy, pair):
        return wt.at[cc, yy, :, :, pl.ds(mm(pair * 256, 256), 256)]

    def w_half(yy, g, pair):
        return wt.at[c, yy, g, :, pl.ds(mm(pair * 256, 256), 256)]

    def to_core(yy, pair):
        push(w_part(c, yy, pair), w_part(c, yy, pair), core_recv + pair * NY + yy, sib)

    def w_round(n):
        pair = pairs[n]
        for zk in ([z + 1 - 2 * (z % 2)] if n == 0 else [pair * 2, pair * 2 + 1]):
            arrived(wt.at[c, y, :, :, pl.ds(mm(zk * 128), 128)], w_recv + zk)
        push(w_part(c, y, pair), w_part(c, y, pair), wy[n], y_up)
        push(w_part(c, y, pair), w_part(c, y, pair), wy[n] + 1, y_dn)
        to_core(y, pair)

    def w_relay(n):
        pair = pairs[n]
        arrived(w_part(c, y3, pair), wy[n])
        push(w_half(y3, 0, pair), w_half(y3, 0, pair), wy[n] + 2, y_up)
        arrived(w_part(c, y1, pair), wy[n] + 1)
        push(w_half(y1, 1, pair), w_half(y1, 1, pair), wy[n] + 3, y_dn)
        to_core(y3, pair)
        to_core(y1, pair)

    def w_last(n):
        pair = pairs[n]
        arrived(w_half(y2, 0, pair), wy[n] + 2)
        arrived(w_half(y2, 1, pair), wy[n] + 3)
        to_core(y2, pair)

    def w_from_core():
        for pair in pairs:
            for yy in (y, y3, y1, y2):
                arrived(w_part(1 - c, yy, pair), core_recv + pair * NY + yy)

    hid_recv = rsem.take(NZ * NC)

    def forward(blocks):
        tokens = jnp.concatenate([ab[b] for b in blocks], axis=0)
        total = jnp.zeros((448, 256), F32)
        for yy in range(NY):
            total = total + dot_nt(wt[:, yy].reshape(448, CHUNK),
                                   tokens[:, yy * CHUNK:(yy + 1) * CHUNK])
        for cc in range(NC):
            for i, b in enumerate(blocks):
                lanes = pl.ds(mm(b * BLK), BLK)
                gate = total[cc * 224:cc * 224 + 112, i * BLK:(i + 1) * BLK]
                up = total[cc * 224 + 112:cc * 224 + 224, i * BLK:(i + 1) * BLK]
                gu[cc, 0, :, lanes] = gate
                gu[cc, 1, :, lanes] = up
                hs[cc, :, lanes] = (gate * jax.nn.sigmoid(gate) * up).astype(BF)

    def backward(blocks):
        for cc in range(NC):
            for b in blocks:
                lanes = pl.ds(mm(b * BLK), BLK)
                gate, up = gu[cc, 0, :, lanes], gu[cc, 1, :, lanes]
                sig = jax.nn.sigmoid(gate)
                silu = gate * sig
                incoming = cb[cc, :, lanes].astype(F32)
                dg[cc, 0:112, lanes] = (incoming * up * sig * (1.0 + gate * (1.0 - sig))).astype(BF)
                dg[cc, 112:224, lanes] = (incoming * silu).astype(BF)

    def hidden_out(k):
        zk = (z + k) % NZ
        for e in range(NC):
            ck = (c + e) % NC
            src = hs.at[ck, :, pl.ds(mm(zk * BLK), BLK)]
            dst = hr.at[pl.ds(mm(z * EIGHTH, 16), EIGHTH), pl.ds(mm(c * BLK), BLK)]
            if k == 0 and e == 0:
                own = pltpu.make_async_copy(src, dst, load_sems.at[5])
                own.start()
                own.wait()
            else:
                push(src, dst, hid_recv + z * NC + c, dev(x, ck, y, zk))

    def blocks_of(step):
        return [ring_block(step, 0), ring_block(step, 1) if step < 4 else z]

    def cot_in():
        cot_push(0, 0)
        for k in range(NZ):
            zk = (z + k) % NZ
            for e in range(NC):
                if k == 0 and e == 0:
                    continue
                ck = (c + e) % NC
                arrived(cb.at[ck, :, pl.ds(mm(zk * BLK), BLK)], cot_recv + zk * NC + ck)

    w_out(1)
    w_out(3)
    w_out(2)
    ring(2, 0)
    w_round(2)
    ring(1, 1)
    w_round(1)
    relay(1)
    w_round(0)
    ring(3, 0)
    w_out(4)
    w_relay(1)
    w_relay(2)
    relay(2)
    cot_out(4)
    cot_push(0, 1)
    w_relay(0)
    w_round(3)
    ring(4, 0)
    cot_out(1)
    ring(2, 1)
    w_relay(3)
    w_last(0)
    w_last(1)
    w_last(2)
    relay(3)
    handed(2)
    cot_out(3)
    handed(1)
    w_last(3)
    w_from_core()
    ring(3, 1)
    relay(4)
    forward(blocks_of(1))
    forward(blocks_of(2))
    handed(3)
    forward(blocks_of(3))
    for k in (3, 5, 2, 6, 1, 7):
        hidden_out(k)
    cot_in()
    backward(blocks_of(1))
    backward(blocks_of(2))
    backward(blocks_of(3))
    ring_wait(4, 1)
    handed(4)
    forward(blocks_of(4))
    backward(blocks_of(4))
    order = [y2, y1, y3, y]
    parts = [(z // 2 + k) % (NZ // 2) for k in (2, 1, 3, 0)]
    core_sum = [[rsem.take() for _ in order] for _ in parts]
    sem_b = [[rsem.take(), rsem.take()] for _ in parts]
    sem_c = [[rsem.take(), rsem.take()] for _ in parts]
    g_recv = rsem.take(NZ)

    def lanes_of(pair):
        return pl.ds(mm(pair * 256, 256), 256)

    def gradient(p, n):
        yy = order[n]
        width = ab[:, :, pl.ds(mm(yy * CHUNK + parts[p] * 256, 256), 256)].reshape(TOK, 256)
        cs[p, n] = dot(dg[1 - c], width).astype(BF).reshape(2, EIGHTH, 256)
        push(cs.at[p, n], cx.at[p, n], core_sum[p][n], sib)
        pa[p, n] = dot(dg[c], width).reshape(2, EIGHTH, 256)

    def send_b(p):
        arrived(cx.at[p, 0], core_sum[p][0])
        rb_send[p] = (pa[p, 0] + cx[p, 0].astype(F32)).astype(BF)
        push(rb_send.at[p, 0], rb.at[p, 0], sem_b[p][0], y_up)
        push(rb_send.at[p, 1], rb.at[p, 1], sem_b[p][1], y_dn)

    def send_c(p):
        for way in range(2):
            n = 1 + way
            arrived(cx.at[p, n], core_sum[p][n])
            rc_send[p, way, 1 - way] = (pa[p, n, 1 - way] + cx[p, n, 1 - way].astype(F32)).astype(BF)
            arrived(rb.at[p, way], sem_b[p][way])
            rc_send[p, way, way] = (
                pa[p, n, way] + cx[p, n, way].astype(F32) + rb[p, way].astype(F32)).astype(BF)
            push(rc_send.at[p, way], rc.at[p, way], sem_c[p][way], y_up if way == 0 else y_dn)

    def send_g(p):
        arrived(cx.at[p, 3], core_sum[p][3])
        total = pa[p, 3] + cx[p, 3].astype(F32)
        for way in range(2):
            arrived(rc.at[p, way], sem_c[p][way])
            total = total + rc[p, way].astype(F32)
        fg[:, :, lanes_of(parts[p])] = total.astype(BF)
        for i in range(2):
            zk = parts[p] * 2 + i
            src = fg.at[:, :, pl.ds(mm(zk * 128), 128)]
            dst = gr.at[:, pl.ds(mm(z * EIGHTH, 16), EIGHTH), :]
            if p < 3:
                push(src, dst, g_recv + z, dev(x, c, y, zk))
        if p == 3:
            zk = z + 1 - 2 * (z % 2)
            push(fg.at[:, :, pl.ds(mm(zk * 128), 128)],
                 gr.at[:, pl.ds(mm(z * EIGHTH, 16), EIGHTH), :], g_recv + z, dev(x, c, y, zk))
            own = pltpu.make_async_copy(fg.at[:, :, pl.ds(mm(z * 128), 128)],
                                        gr.at[:, pl.ds(mm(z * EIGHTH, 16), EIGHTH), :], load_sems.at[5])
            own.start()
            own.wait()

    gradient(0, 0)
    gradient(2, 2)
    gradient(1, 0)
    gradient(2, 0)
    gradient(0, 1)
    send_b(0)
    gradient(0, 2)
    send_b(1)
    gradient(1, 2)
    hidden_out(4)
    send_b(2)
    gradient(1, 1)
    send_c(0)
    gradient(0, 3)
    gradient(3, 0)
    gradient(2, 1)
    send_c(1)
    gradient(3, 1)
    gradient(3, 2)
    send_b(3)
    send_g(0)
    send_c(2)
    gradient(1, 3)
    hidden_out(0)
    gradient(2, 3)
    send_c(3)
    send_g(1)
    gradient(3, 3)
    send_g(2)
    send_g(3)

    for k in range(NZ):
        zk = (z + k) % NZ
        for e in range(NC):
            if k == 0 and e == 0:
                continue
            ck = (c + e) % NC
            arrived(hr.at[pl.ds(mm(zk * EIGHTH, 16), EIGHTH), pl.ds(mm(ck * BLK), BLK)],
                    hid_recv + zk * NC + ck)
    for k in range(1, NZ):
        zk = (z + k) % NZ
        arrived(gr.at[:, pl.ds(mm(zk * EIGHTH, 16), EIGHTH), :], g_recv + zk)
    def drain(k, _):
        own_copy((t + k) % NT).wait_send()
        return 0

    lax.fori_loop(1, NT, drain, 0)
    for copy in started:
        copy.wait_send()
    assert ssem.n <= send_sems.shape[0] and rsem.n <= recv_sems.shape[0], (ssem.n, rsem.n)


def per_device(activations, cotangent, old_gate_up, kept_index, new_slot):
    any_ = pl.BlockSpec(memory_space=pl.ANY)
    vmem = pl.BlockSpec(memory_space=pltpu.VMEM)
    V = pltpu.VMEM
    raw = pl.pallas_call(
        kernel,
        out_shape=(
            jax.ShapeDtypeStruct((OWN, 256), BF),
            jax.ShapeDtypeStruct((OWN, 256), BF),
            jax.ShapeDtypeStruct((2, OWN, 128), BF),
        ),
        in_specs=[any_] * 5,
        out_specs=(vmem, vmem, vmem),
        scratch_shapes=[
            V((BLK, D), BF),
            V((256, OWN), BF),
            V((128, 2, ROWS), BF),
            V((256, ROWS), BF),
            V((1, KEEP), jnp.int32),
            V((1, KEEP), jnp.int32),
            V((NZ, BLK, D), BF),
            V((8, KEEP), jnp.int32),
            V((KB * 16, 128), BF),
            V((KB * 16, 128), F32),
            V((CAP, ROWS), BF),
            V((NT, CAP, 256), BF),
            V((PLACES, 256), BF),
            V((2, OWN, 128), BF),
            V((NC, NY, 2, EIGHTH, CHUNK), BF),
            V((OWN, 256), BF),
            V((NC, EIGHTH, TOK), BF),
            V((NC, EIGHTH, TOK), BF),
            V((NC, 2, EIGHTH, TOK), F32),
            V((NC, 2 * EIGHTH, TOK), BF),
            V((4, NY, 2, EIGHTH, 256), BF),
            V((4, NY, 2, EIGHTH, 256), BF),
            V((4, NY, 2, EIGHTH, 256), F32),
            V((4, 2, EIGHTH, 256), BF),
            V((4, 2, EIGHTH, 256), BF),
            V((4, 2, 2, EIGHTH, 256), BF),
            V((4, 2, 2, EIGHTH, 256), BF),
            V((2, EIGHTH, CHUNK), BF),
            pltpu.SemaphoreType.DMA((6,)),
            pltpu.SemaphoreType.DMA((224,)),
            pltpu.SemaphoreType.DMA((224,)),
        ],
        compiler_params=pltpu.CompilerParams(
            collective_id=0, has_side_effects=True, vmem_limit_bytes=60 * 1024 * 1024),
        cost_estimate=pl.CostEstimate(flops=12_000_000_000, bytes_accessed=8_000_000, transcendentals=1_000_000),
        name="student_projection",
    )(activations, cotangent, old_gate_up,
      kept_index.reshape(1, KEEP), new_slot.reshape(1, KEEP))
    return pl.pallas_call(
        finish,
        out_shape=(
            jax.ShapeDtypeStruct((128, 2, OWN), BF),
            jax.ShapeDtypeStruct((256, OWN), BF),
            jax.ShapeDtypeStruct((128, 2, OWN), BF),
        ),
        in_specs=[any_] * 3,
        out_specs=(any_,) * 3,
        scratch_shapes=[
            V((OWN, 256), BF), V((OWN, 256), BF), V((2, OWN, 128), BF),
            V((128, 2, OWN), BF), V((256, OWN), BF), V((128, 2, OWN), BF),
            pltpu.SemaphoreType.DMA((6,)),
        ],
        compiler_params=pltpu.CompilerParams(vmem_limit_bytes=60 * 1024 * 1024),
        name="finish",
    )(*raw)


def solution(mesh):
    placed = (P("dp", None), P("dp", "tensor"), P("dp", None, "tensor"), P(), P())
    return jax.shard_map(
        per_device,
        mesh=mesh,
        in_specs=placed,
        out_specs=(P("dp", None, "tensor"), P("dp", "tensor"), P("dp", None, "tensor")),
        check_vma=False,
    )
```

```python
import jax
import jax.numpy as jnp
from jax import lax
from jax.experimental import pallas as pl
from jax.experimental.pallas import tpu as pltpu
from jax.sharding import PartitionSpec as P

MESH = pl.DeviceIdType.MESH
NZ, NY, NX, NC = 8, 4, 4, 2
NT = NX * NC
D = 4096
KEEP = 7168
OWN = 896
ROWS = 3584
CAP = 176
PLACES = NT * CAP
EIGHTH = OWN // NZ
BLK = 128
TOK = NZ * BLK
CHUNK = D // NY
DIRECT = 1024
SHARE = (D - DIRECT) // NX
HALF = BLK // 2
KB = KEEP // 128
F32 = jnp.float32
BF = jnp.bfloat16


def iota(shape, dim):
    return lax.broadcasted_iota(jnp.int32, shape, dim)


def dot(a, b):
    return lax.dot_general(a, b, (((1,), (0,)), ((), ())), preferred_element_type=F32)


def dot_nt(a, b):
    return lax.dot_general(a, b, (((1,), (1,)), ((), ())), preferred_element_type=F32)


def onehot(cond):
    return jnp.where(cond, 1.0, 0.0).astype(BF)


def interleave_matrix():
    a = iota((256, 256), 0)
    return onehot(iota((256, 256), 1) == (a & 1) * 128 + (a >> 1))


def mm(i, m=128):
    return pl.multiple_of(i, m)


class Sems:
    def __init__(self, ref):
        self.ref, self.n = ref, 0

    def take(self, count=1):
        first = self.n
        self.n += count
        return first


def finish(stn, hr, gr, stu, hid, wg, stn_v, hr_v, gr_v, stu_v, hid_v, wg_v, sems):
    loads = [pltpu.make_async_copy(a, b, sems.at[i])
             for i, (a, b) in enumerate(((stn, stn_v), (hr, hr_v), (gr, gr_v)))]
    stores = [pltpu.make_async_copy(a, b, sems.at[i + 3])
              for i, (a, b) in enumerate(((stu_v, stu), (hid_v, hid), (wg_v, wg)))]
    for load in loads:
        load.start()
    loads[0].wait()
    stu_v[...] = stn_v[...].astype(F32).T.astype(BF).reshape(128, 2, OWN)
    stores[0].start()
    loads[1].wait()
    hid_v[...] = hr_v[...].astype(F32).T.astype(BF)
    stores[1].start()
    loads[2].wait()
    both = jnp.concatenate([gr_v[0], gr_v[1]], axis=1)
    wg_v[...] = dot_nt(interleave_matrix(), both).astype(BF).reshape(128, 2, OWN)
    stores[2].start()
    for store in stores:
        store.wait()


def kernel(act, cot, old, kept, slot, stn, hr, gr,
           a_in, c_in, o_in, o_two, krow, srow, ab, idx, ohs, inc, pb, rts, rr, st2, wt, ct, cb,
           hs, gu, dg, cs, cx, pa, rb_send, rb, rc_send, rc, fg,
           load_sems, send_sems, recv_sems):
    dp = lax.axis_index("dp")
    t = lax.axis_index("tensor")
    z, y = dp // NY, dp % NY
    x, c = t // NC, t % NC

    def dev(x_, c_, y_, z_):
        return (z_ * NY + y_, x_ * NC + c_)

    sib = dev(x, 1 - c, y, z)
    z_up, z_dn = dev(x, c, y, (z + 1) % NZ), dev(x, c, y, (z + NZ - 1) % NZ)
    y_up, y_dn = dev(x, c, (y + 1) % NY, z), dev(x, c, (y + NY - 1) % NY, z)
    x_up, x_dn = dev((x + 1) % NX, c, y, z), dev((x + NX - 1) % NX, c, y, z)

    ssem, rsem = Sems(send_sems), Sems(recv_sems)
    started = []

    def push(src, dst, recv, device):
        copy = pltpu.make_async_remote_copy(
            src_ref=src, dst_ref=dst, send_sem=send_sems.at[ssem.take()],
            recv_sem=recv_sems.at[recv], device_id=device, device_id_type=MESH)
        copy.start()
        started.append(copy)

    def arrived(dst, recv):
        pltpu.make_async_remote_copy(
            src_ref=dst, dst_ref=dst, send_sem=send_sems.at[0],
            recv_sem=recv_sems.at[recv], device_id=sib, device_id_type=MESH).wait_recv()

    partners = []
    for k in range(1, NT):
        tk = (t + k) % NT
        partners.append((dp, tk))
    for k in range(1, NZ):
        zk = (z + k) % NZ
        partners.append(dev(x, c, y, zk))
        partners.append(dev(x, 1 - c, y, zk))
    partners.append(y_up)
    partners.append(y_dn)
    barrier = pltpu.get_barrier_semaphore()
    for p in partners:
        pl.semaphore_signal(barrier, inc=1, device_id=p, device_id_type=MESH)

    loads = [
        pltpu.make_async_copy(act.at[pl.ds(mm(c * BLK), BLK), :], a_in, load_sems.at[0]),
        pltpu.make_async_copy(cot, c_in, load_sems.at[1]),
        pltpu.make_async_copy(kept, krow, load_sems.at[2]),
        pltpu.make_async_copy(slot, srow, load_sems.at[3]),
        pltpu.make_async_copy(old, o_in, load_sems.at[4]),
    ]
    for load in loads:
        load.start()

    loads[0].wait()
    for yy in range(NY):
        for zz in range(NZ):
            ab[z, :, yy * CHUNK + zz * 128:yy * CHUNK + (zz + 1) * 128] = (
                a_in[:, (zz * NY + yy) * 128:(zz * NY + yy + 1) * 128])

    def share(xx):
        return pl.ds(mm(DIRECT + xx % NX * SHARE), SHARE)

    regions = [share(x), pl.ds(0, DIRECT)]
    ring_recv = [[[rsem.take(), rsem.take()] for _ in range(2)] for _ in range(4)]
    hand_recv = [[rsem.take(4), rsem.take(4)] for _ in range(4)]

    def ring_block(step, way):
        return (z + NZ - step) % NZ if way == 0 else (z + step) % NZ

    def ring_rows(step, way):
        if step < 4:
            return pl.ds(0, BLK)
        return pl.ds(0, HALF) if way == 0 else pl.ds(HALF, HALF)

    def ring_send(step, r):
        for way in range(2):
            piece = ab.at[ring_block(step - 1, way), ring_rows(step, way), regions[r]]
            push(piece, piece, ring_recv[step - 1][way][r], z_up if way == 0 else z_dn)

    def ring_wait(step, r):
        for way in range(2):
            arrived(ab.at[ring_block(step, way), ring_rows(step, way), regions[r]],
                    ring_recv[step - 1][way][r])

    def hand_blocks(step):
        return [(ring_block(step, way), hand_recv[step - 1][way]) for way in range(2 if step < 4 else 1)]

    def hand_on(step):
        for block, sem in hand_blocks(step):
            piece = ab.at[block, :, share(x)]
            push(piece, piece, sem, x_up)
            push(piece, piece, sem + 1, x_dn)

    def relay(step):
        for block, sem in hand_blocks(step):
            arrived(ab.at[block, :, share(x + 3)], sem)
            piece = ab.at[block, pl.ds(0, HALF), share(x + 3)]
            push(piece, piece, sem + 2, x_up)
            arrived(ab.at[block, :, share(x + 1)], sem + 1)
            piece = ab.at[block, pl.ds(HALF, HALF), share(x + 1)]
            push(piece, piece, sem + 3, x_dn)

    def handed(step):
        for block, sem in hand_blocks(step):
            arrived(ab.at[block, pl.ds(0, HALF), share(x + 2)], sem + 2)
            arrived(ab.at[block, pl.ds(HALF, HALF), share(x + 2)], sem + 3)

    def ring(step, r):
        ring_wait(step, r)
        if step < 4:
            ring_send(step + 1, r)
        if r == 0:
            hand_on(step)

    loads[1].wait()
    ct[...] = c_in[...].astype(F32).T.astype(BF)
    cot_recv = rsem.take(NZ * NC)
    cot_slot = cot_recv + z * NC + c

    def cot_push(k, e):
        zk, ck = (z + k) % NZ, (c + e) % NC
        src = ct.at[pl.ds(mm(zk * EIGHTH, 16), EIGHTH), pl.ds(mm(ck * BLK), BLK)]
        dst = cb.at[c, :, pl.ds(mm(z * BLK), BLK)]
        if k == 0 and e == 0:
            own = pltpu.make_async_copy(src, dst, load_sems.at[5])
            own.start()
            own.wait()
        else:
            push(src, dst, cot_slot, dev(x, ck, y, zk))

    def both_ways(k):
        return (k, NZ - k) if k < 4 else (4,)

    def cot_out(distance):
        for k in both_ways(distance):
            for e in range(NC):
                cot_push(k, e)

    loads[2].wait()
    loads[3].wait()
    kv, sv = krow[...], srow[...]
    o, j = jnp.zeros_like(kv), jnp.zeros_like(sv)
    for i in range(1, NT):
        o = o + jnp.where(kv >= ROWS * i, 1, 0)
        j = j + jnp.where(sv >= OWN * i, 1, 0)
    idx[0:1, :] = jnp.where(o == t, j, 99)
    idx[1:2, :] = jnp.where(j == t, o + 8, 99)
    row16 = iota((16, 128), 0)
    for b in range(KB):
        lanes = slice(b * 128, (b + 1) * 128)
        key = jnp.where(row16 < 8, jnp.broadcast_to(idx[0:1, lanes], (16, 128)),
                        jnp.broadcast_to(idx[1:2, lanes], (16, 128)))
        ohs[b * 16:(b + 1) * 16, :] = onehot(key == row16)
    upto = onehot(iota((128, 128), 0) <= iota((128, 128), 1))
    inc[...] = dot(ohs[...], upto)
    run = jnp.zeros((16, 1), F32)
    for b in range(KB):
        lanes = slice(b * 128, (b + 1) * 128)
        here = inc[b * 16:(b + 1) * 16, :]
        rank = ohs[b * 16:(b + 1) * 16, :].astype(F32) * (here + run)
        rank_s = jnp.sum(rank[0:8], axis=0, keepdims=True).astype(jnp.int32)
        rank_r = jnp.sum(rank[8:16], axis=0, keepdims=True).astype(jnp.int32)
        dest, source = idx[0:1, lanes], idx[1:2, lanes]
        idx[2:3, lanes] = jnp.where(dest < 99, dest * CAP + rank_s, 0)
        idx[3:4, lanes] = jnp.where(source < 99, (source - 8) * CAP + rank_r, 0)
        run = run + here[:, 127:128]
    idx[4:5, :] = kv - t * ROWS
    idx[5:6, :] = sv - t * OWN

    def scatter(step, carry):
        by_neuron, by_slot = carry
        lanes = pl.ds(mm(step * OWN), OWN)
        vs, vr, ln, ls = (idx[i:i + 1, lanes] for i in (2, 3, 4, 5))
        high = iota((32, OWN), 0) == (ln >> 7)
        values = jnp.concatenate([
            jnp.where(high, vs >> 7, 0), jnp.where(high, vs & 127, 0)], axis=0)
        low = onehot(iota((128, OWN), 0) == (ln & 127))
        by_neuron = by_neuron + dot_nt(values.astype(F32).astype(BF), low)
        high = iota((8, OWN), 0) == (ls >> 7)
        values = jnp.concatenate([
            jnp.where(high, vr >> 7, 0), jnp.where(high, vr & 127, 0)], axis=0)
        low = onehot(iota((128, OWN), 0) == (ls & 127))
        by_slot = by_slot + dot_nt(low, values.astype(F32).astype(BF))
        return by_neuron, by_slot

    by_neuron, by_slot = lax.fori_loop(
        0, KEEP // OWN, scatter, (jnp.zeros((64, 128), F32), jnp.zeros((128, 16), F32)))
    place_s = (by_neuron[0:32] * 128.0 + by_neuron[32:64]).astype(jnp.int32)
    place_r = (by_slot[:, 0:8] * 128.0 + by_slot[:, 8:16]).astype(jnp.int32)

    loads[4].wait()
    o_two[...] = o_in[...].reshape(256, ROWS)

    pl.semaphore_wait(barrier, len(partners))
    ring_send(1, 0)
    ring_send(1, 1)
    own_recv = rsem.take(NT)
    own_send = ssem.take(NT)

    def own_copy(to):
        return pltpu.make_async_remote_copy(
            src_ref=rts.at[to], dst_ref=rr.at[pl.ds(mm(t * CAP, 16), CAP), :],
            send_sem=send_sems.at[own_send + to], recv_sem=recv_sems.at[own_recv + t],
            device_id=(dp, to), device_id_type=MESH)

    def select(k, _):
        row = iota((2 * CAP, 128), 0) + (k * (2 * CAP) + 1)
        for h in range(ROWS // 128):
            pb[:, h * 128:(h + 1) * 128] = onehot(place_s[h:h + 1, :] == row)
        rts[pl.ds(2 * k, 2)] = dot_nt(pb[...], o_two[...]).astype(BF).reshape(2, CAP, 256)
        return 0

    lax.fori_loop(0, NT // 2, select, 0)

    def own_start(k, _):
        own_copy((t + k) % NT).start()
        return 0

    lax.fori_loop(1, NT, own_start, 0)
    rr[pl.ds(mm(t * CAP, 16), CAP), :] = rts[t]

    cot_out(2)
    ring(1, 0)
    for k in range(1, NT):
        frm = (t + k) % NT
        arrived(rr.at[pl.ds(mm(frm * CAP, 16), CAP), :], own_recv + frm)
    pi = interleave_matrix()
    got = rr[...]
    for h in range(OWN // 128):
        q = onehot(iota((128, PLACES), 1) + 1 == place_r[:, h:h + 1])
        mine = dot(q, got).astype(BF)
        stn[h * 128:(h + 1) * 128, :] = mine
        split = dot(mine, pi).astype(BF)
        st2[0, h * 128:(h + 1) * 128, :] = split[:, 0:128]
        st2[1, h * 128:(h + 1) * 128, :] = split[:, 128:256]

    w_recv = rsem.take(NZ)

    def eighth(k):
        zk = (z + k) % NZ
        return (st2.at[:, pl.ds(mm(zk * EIGHTH, 16), EIGHTH), :],
                wt.at[c, y, :, :, pl.ds(mm(z * 128), 128)], dev(x, c, y, zk))

    own = pltpu.make_async_copy(*eighth(0)[:2], load_sems.at[5])
    own.start()
    own.wait()

    def w_out(distance):
        for k in both_ways(distance):
            src, dst, to = eighth(k)
            push(src, dst, w_recv + z, to)

    y1, y3, y2 = (y + 1) % NY, (y + 3) % NY, (y + 2) % NY
    pairs = [(z // 2 + k) % (NZ // 2) for k in (0, 1, 3, 2)]
    wy = [rsem.take(4) for _ in pairs]
    core_recv = rsem.take(NY * len(pairs))

    def w_part(cc, yy, pair):
        return wt.at[cc, yy, :, :, pl.ds(mm(pair * 256, 256), 256)]

    def w_half(yy, g, pair):
        return wt.at[c, yy, g, :, pl.ds(mm(pair * 256, 256), 256)]

    def to_core(yy, pair):
        push(w_part(c, yy, pair), w_part(c, yy, pair), core_recv + pair * NY + yy, sib)

    def w_round(n):
        pair = pairs[n]
        for zk in ([z + 1 - 2 * (z % 2)] if n == 0 else [pair * 2, pair * 2 + 1]):
            arrived(wt.at[c, y, :, :, pl.ds(mm(zk * 128), 128)], w_recv + zk)
        push(w_part(c, y, pair), w_part(c, y, pair), wy[n], y_up)
        push(w_part(c, y, pair), w_part(c, y, pair), wy[n] + 1, y_dn)
        to_core(y, pair)

    def w_relay(n):
        pair = pairs[n]
        arrived(w_part(c, y3, pair), wy[n])
        push(w_half(y3, 0, pair), w_half(y3, 0, pair), wy[n] + 2, y_up)
        arrived(w_part(c, y1, pair), wy[n] + 1)
        push(w_half(y1, 1, pair), w_half(y1, 1, pair), wy[n] + 3, y_dn)
        to_core(y3, pair)
        to_core(y1, pair)

    def w_last(n):
        pair = pairs[n]
        arrived(w_half(y2, 0, pair), wy[n] + 2)
        arrived(w_half(y2, 1, pair), wy[n] + 3)
        to_core(y2, pair)

    def w_from_core():
        for pair in pairs:
            for yy in (y, y3, y1, y2):
                arrived(w_part(1 - c, yy, pair), core_recv + pair * NY + yy)

    hid_recv = rsem.take(NZ * NC)

    def forward(blocks):
        tokens = jnp.concatenate([ab[b] for b in blocks], axis=0)
        total = jnp.zeros((448, 256), F32)
        for yy in range(NY):
            total = total + dot_nt(wt[:, yy].reshape(448, CHUNK),
                                   tokens[:, yy * CHUNK:(yy + 1) * CHUNK])
        for cc in range(NC):
            for i, b in enumerate(blocks):
                lanes = pl.ds(mm(b * BLK), BLK)
                gate = total[cc * 224:cc * 224 + 112, i * BLK:(i + 1) * BLK]
                up = total[cc * 224 + 112:cc * 224 + 224, i * BLK:(i + 1) * BLK]
                gu[cc, 0, :, lanes] = gate
                gu[cc, 1, :, lanes] = up
                hs[cc, :, lanes] = (gate * jax.nn.sigmoid(gate) * up).astype(BF)

    def backward(blocks):
        for cc in range(NC):
            for b in blocks:
                lanes = pl.ds(mm(b * BLK), BLK)
                gate, up = gu[cc, 0, :, lanes], gu[cc, 1, :, lanes]
                sig = jax.nn.sigmoid(gate)
                silu = gate * sig
                incoming = cb[cc, :, lanes].astype(F32)
                dg[cc, 0:112, lanes] = (incoming * up * sig * (1.0 + gate * (1.0 - sig))).astype(BF)
                dg[cc, 112:224, lanes] = (incoming * silu).astype(BF)

    def hidden_out(k):
        zk = (z + k) % NZ
        for e in range(NC):
            ck = (c + e) % NC
            src = hs.at[ck, :, pl.ds(mm(zk * BLK), BLK)]
            dst = hr.at[pl.ds(mm(z * EIGHTH, 16), EIGHTH), pl.ds(mm(c * BLK), BLK)]
            if k == 0 and e == 0:
                own = pltpu.make_async_copy(src, dst, load_sems.at[5])
                own.start()
                own.wait()
            else:
                push(src, dst, hid_recv + z * NC + c, dev(x, ck, y, zk))

    def blocks_of(step):
        return [ring_block(step, 0), ring_block(step, 1) if step < 4 else z]

    def cot_in():
        cot_push(0, 0)
        for k in range(NZ):
            zk = (z + k) % NZ
            for e in range(NC):
                if k == 0 and e == 0:
                    continue
                ck = (c + e) % NC
                arrived(cb.at[ck, :, pl.ds(mm(zk * BLK), BLK)], cot_recv + zk * NC + ck)

    w_out(1)
    w_out(3)
    w_out(2)
    ring(2, 0)
    w_round(2)
    ring(1, 1)
    w_round(1)
    relay(1)
    w_round(0)
    ring(3, 0)
    w_out(4)
    w_relay(1)
    w_relay(2)
    relay(2)
    cot_out(4)
    cot_push(0, 1)
    w_relay(0)
    w_round(3)
    ring(4, 0)
    cot_out(1)
    ring(2, 1)
    w_relay(3)
    w_last(0)
    w_last(1)
    w_last(2)
    relay(3)
    handed(2)
    cot_out(3)
    handed(1)
    w_last(3)
    w_from_core()
    ring(3, 1)
    relay(4)
    forward(blocks_of(1))
    forward(blocks_of(2))
    handed(3)
    forward(blocks_of(3))
    for k in (3, 5, 2, 6, 1, 7):
        hidden_out(k)
    cot_in()
    backward(blocks_of(1))
    backward(blocks_of(2))
    backward(blocks_of(3))
    ring_wait(4, 1)
    handed(4)
    forward(blocks_of(4))
    backward(blocks_of(4))
    order = [y2, y1, y3, y]
    parts = [(z // 2 + k) % (NZ // 2) for k in (2, 1, 3, 0)]
    core_sum = [[rsem.take() for _ in order] for _ in parts]
    sem_b = [[rsem.take(), rsem.take()] for _ in parts]
    sem_c = [[rsem.take(), rsem.take()] for _ in parts]
    g_recv = rsem.take(NZ)

    def lanes_of(pair):
        return pl.ds(mm(pair * 256, 256), 256)

    def gradient(p, n):
        yy = order[n]
        width = ab[:, :, pl.ds(mm(yy * CHUNK + parts[p] * 256, 256), 256)].reshape(TOK, 256)
        cs[p, n] = dot(dg[1 - c], width).astype(BF).reshape(2, EIGHTH, 256)
        push(cs.at[p, n], cx.at[p, n], core_sum[p][n], sib)
        pa[p, n] = dot(dg[c], width).reshape(2, EIGHTH, 256)

    def send_b(p):
        arrived(cx.at[p, 0], core_sum[p][0])
        rb_send[p] = (pa[p, 0] + cx[p, 0].astype(F32)).astype(BF)
        push(rb_send.at[p, 0], rb.at[p, 0], sem_b[p][0], y_up)
        push(rb_send.at[p, 1], rb.at[p, 1], sem_b[p][1], y_dn)

    def send_c(p):
        for way in range(2):
            n = 1 + way
            arrived(cx.at[p, n], core_sum[p][n])
            rc_send[p, way, 1 - way] = (pa[p, n, 1 - way] + cx[p, n, 1 - way].astype(F32)).astype(BF)
            arrived(rb.at[p, way], sem_b[p][way])
            rc_send[p, way, way] = (
                pa[p, n, way] + cx[p, n, way].astype(F32) + rb[p, way].astype(F32)).astype(BF)
            push(rc_send.at[p, way], rc.at[p, way], sem_c[p][way], y_up if way == 0 else y_dn)

    def send_g(p):
        arrived(cx.at[p, 3], core_sum[p][3])
        total = pa[p, 3] + cx[p, 3].astype(F32)
        for way in range(2):
            arrived(rc.at[p, way], sem_c[p][way])
            total = total + rc[p, way].astype(F32)
        fg[:, :, lanes_of(parts[p])] = total.astype(BF)
        for i in range(2):
            zk = parts[p] * 2 + i
            src = fg.at[:, :, pl.ds(mm(zk * 128), 128)]
            dst = gr.at[:, pl.ds(mm(z * EIGHTH, 16), EIGHTH), :]
            if p < 3:
                push(src, dst, g_recv + z, dev(x, c, y, zk))
        if p == 3:
            zk = z + 1 - 2 * (z % 2)
            push(fg.at[:, :, pl.ds(mm(zk * 128), 128)],
                 gr.at[:, pl.ds(mm(z * EIGHTH, 16), EIGHTH), :], g_recv + z, dev(x, c, y, zk))
            own = pltpu.make_async_copy(fg.at[:, :, pl.ds(mm(z * 128), 128)],
                                        gr.at[:, pl.ds(mm(z * EIGHTH, 16), EIGHTH), :], load_sems.at[5])
            own.start()
            own.wait()

    gradient(0, 0)
    gradient(2, 2)
    gradient(1, 0)
    gradient(2, 0)
    gradient(0, 1)
    send_b(0)
    gradient(0, 2)
    send_b(1)
    gradient(1, 2)
    hidden_out(4)
    send_b(2)
    gradient(1, 1)
    send_c(0)
    gradient(0, 3)
    gradient(3, 0)
    gradient(2, 1)
    send_c(1)
    gradient(3, 1)
    gradient(3, 2)
    send_b(3)
    send_g(0)
    send_c(2)
    gradient(1, 3)
    hidden_out(0)
    gradient(2, 3)
    send_c(3)
    send_g(1)
    gradient(3, 3)
    send_g(2)
    send_g(3)

    for k in range(NZ):
        zk = (z + k) % NZ
        for e in range(NC):
            if k == 0 and e == 0:
                continue
            ck = (c + e) % NC
            arrived(hr.at[pl.ds(mm(zk * EIGHTH, 16), EIGHTH), pl.ds(mm(ck * BLK), BLK)],
                    hid_recv + zk * NC + ck)
    for k in range(1, NZ):
        zk = (z + k) % NZ
        arrived(gr.at[:, pl.ds(mm(zk * EIGHTH, 16), EIGHTH), :], g_recv + zk)
    def drain(k, _):
        own_copy((t + k) % NT).wait_send()
        return 0

    lax.fori_loop(1, NT, drain, 0)
    for copy in started:
        copy.wait_send()
    assert ssem.n <= send_sems.shape[0] and rsem.n <= recv_sems.shape[0], (ssem.n, rsem.n)


def per_device(activations, cotangent, old_gate_up, kept_index, new_slot):
    any_ = pl.BlockSpec(memory_space=pl.ANY)
    vmem = pl.BlockSpec(memory_space=pltpu.VMEM)
    V = pltpu.VMEM
    raw = pl.pallas_call(
        kernel,
        out_shape=(
            jax.ShapeDtypeStruct((OWN, 256), BF),
            jax.ShapeDtypeStruct((OWN, 256), BF),
            jax.ShapeDtypeStruct((2, OWN, 128), BF),
        ),
        in_specs=[any_] * 5,
        out_specs=(vmem, vmem, vmem),
        scratch_shapes=[
            V((BLK, D), BF),
            V((256, OWN), BF),
            V((128, 2, ROWS), BF),
            V((256, ROWS), BF),
            V((1, KEEP), jnp.int32),
            V((1, KEEP), jnp.int32),
            V((NZ, BLK, D), BF),
            V((8, KEEP), jnp.int32),
            V((KB * 16, 128), BF),
            V((KB * 16, 128), F32),
            V((2 * CAP, ROWS), BF),
            V((NT, CAP, 256), BF),
            V((PLACES, 256), BF),
            V((2, OWN, 128), BF),
            V((NC, NY, 2, EIGHTH, CHUNK), BF),
            V((OWN, 256), BF),
            V((NC, EIGHTH, TOK), BF),
            V((NC, EIGHTH, TOK), BF),
            V((NC, 2, EIGHTH, TOK), F32),
            V((NC, 2 * EIGHTH, TOK), BF),
            V((4, NY, 2, EIGHTH, 256), BF),
            V((4, NY, 2, EIGHTH, 256), BF),
            V((4, NY, 2, EIGHTH, 256), F32),
            V((4, 2, EIGHTH, 256), BF),
            V((4, 2, EIGHTH, 256), BF),
            V((4, 2, 2, EIGHTH, 256), BF),
            V((4, 2, 2, EIGHTH, 256), BF),
            V((2, EIGHTH, CHUNK), BF),
            pltpu.SemaphoreType.DMA((6,)),
            pltpu.SemaphoreType.DMA((224,)),
            pltpu.SemaphoreType.DMA((224,)),
        ],
        compiler_params=pltpu.CompilerParams(
            collective_id=0, has_side_effects=True, vmem_limit_bytes=60 * 1024 * 1024),
        cost_estimate=pl.CostEstimate(flops=12_000_000_000, bytes_accessed=8_000_000, transcendentals=1_000_000),
        name="student_projection",
    )(activations, cotangent, old_gate_up,
      kept_index.reshape(1, KEEP), new_slot.reshape(1, KEEP))
    return pl.pallas_call(
        finish,
        out_shape=(
            jax.ShapeDtypeStruct((128, 2, OWN), BF),
            jax.ShapeDtypeStruct((256, OWN), BF),
            jax.ShapeDtypeStruct((128, 2, OWN), BF),
        ),
        in_specs=[any_] * 3,
        out_specs=(any_,) * 3,
        scratch_shapes=[
            V((OWN, 256), BF), V((OWN, 256), BF), V((2, OWN, 128), BF),
            V((128, 2, OWN), BF), V((256, OWN), BF), V((128, 2, OWN), BF),
            pltpu.SemaphoreType.DMA((6,)),
        ],
        compiler_params=pltpu.CompilerParams(vmem_limit_bytes=60 * 1024 * 1024),
        name="finish",
    )(*raw)


def solution(mesh):
    placed = (P("dp", None), P("dp", "tensor"), P("dp", None, "tensor"), P(), P())
    return jax.shard_map(
        per_device,
        mesh=mesh,
        in_specs=placed,
        out_specs=(P("dp", None, "tensor"), P("dp", "tensor"), P("dp", None, "tensor")),
        check_vma=False,
    )
```
